32 devices in a mesh: groups: 2 (over y), charge: 8 (over z, core), split: 2 (over x).
Axes of the slice: x: 2, y: 2, z: 4, core: 2. Of those that a mesh axis runs over, the one named last changes fastest.
Arguments:
- left_env: bfloat16 [16, 1024, 1024], P(('groups', 'charge'), 'split'), parts along dimension 0, may hold values from -6 to 6
- site_tensor: bfloat16 [16, 4, 1024, 1024], P(('groups', 'charge'), None, None, 'split'), parts along dimension 0, may hold values from -0.1875 to 0.1875
- left_sizes: int32 [16], P(('groups', 'charge')), parts along dimension 0, may hold values from 1 to 1024, 4096 in all
- right_sizes: int32 [16], P('groups'), parts along dimension 0, may hold values from 1 to 1024, 4096 in all
- targets: int32 [16, 4], P(('groups', 'charge')), parts along dimension 0, may hold values from 0 to 7, all different within a row
Outputs:
- new_env: float32 [16, 1024, 1024], P('groups', 'charge', 'split'), parts along dimension 0
The draws below stay inside these ranges and needn't reach their ends.
There are 2 independent parts, one for each index of `groups`. The reference program is written for one: setup_inputs(seed, part) draws one part's arguments, and reference() takes and returns one part's arrays. A program takes and returns all parts, laid end to end along the dimension named above; each array names one. Nothing has to cross between parts.
Inputs may be any that keep to these rules, and one draw needn't show every extreme that they name: `targets`: the 4 entries of one row are distinct, and every right-bond sector is reached by some row. `left_sizes`: they sum to 8 * B // 2 and the largest is exactly 1024. `right_sizes`: they sum to 8 * B // 2 and the largest is exactly 1024.
All inputs are finite; a program needn't handle non-finite values. No bound on the sum of `left_sizes` on one device may be relied on, other than what follows from the above.
Results may differ from the reference program's by a relative error of at most 0.015.
Values may be sent and summed in bfloat16 or wider, within the bound.
No kernel may reach another device: no remote copies, remote signals or barrier semaphores. Data moves between devices by JAX's collectives and lax.ppermute only.
A program may use at most 64 MiB of HBM per device.

```python
import math
import jax
import jax.numpy as jnp
import numpy as np
from jax import lax

B = 1024
PHYS = 4
SECTORS = 8


def level_of(key, dims, cuts, low, high):
    def one(dim, shards_of):
        draws = jax.random.uniform(jax.random.fold_in(jax.random.fold_in(key, 6), dim), (shards_of,), jnp.float32, low / len(cuts), high / len(cuts))
        return jnp.repeat(jnp.exp(draws), dims[dim] // shards_of).reshape((-1,) + (1,) * (len(dims) - dim - 1))

    level = one(*cuts[0])
    for cut in cuts[1:]:
        level = level * one(*cut)
    return level


def distinct(stream_key, rows, number_of, top, lift):
    sequence = jax.random.permutation(jax.random.fold_in(stream_key, 1), number_of)
    boost = sequence
    for power in range(3):
        boost = boost * boost // number_of
    boost = boost * lift // number_of
    chance = jax.random.randint(jax.random.fold_in(stream_key, 2), (rows, number_of), 0, 4096) + boost
    holders = jax.random.permutation(jax.random.fold_in(stream_key, 3), rows)[jnp.arange(number_of) % rows]
    chance = jnp.where(jnp.arange(rows)[:, None] == holders[None, :], 1 << 14, chance)
    score = chance * number_of + jnp.arange(number_of)
    return lax.top_k(score.astype(jnp.int32), top)[1].astype(jnp.int32)


def profile(number_of, total, most, slope):
    loads = [(1 << 20) // math.isqrt(rank ** slope) + 1 for rank in range(2, number_of + 1)]
    surplus, counts = total - most - (number_of - 1), [1] * (number_of - 1)
    while surplus > 0:
        movable = [i for i in range(number_of - 1) if counts[i] < most]
        whole, remaining = sum([loads[i] for i in movable]), surplus
        for i in movable:
            more = min(most - counts[i], max(1, remaining * loads[i] // whole), surplus)
            counts[i] = counts[i] + more
            surplus = surplus - more
    return np.array([most] + counts)


def uneven(rng, number_of, total, reach, slope):
    if number_of == 2:
        one = jax.random.randint(rng, (), max(1, total - reach), min(reach, total - 1) + 1)
        return jnp.stack([one, total - one])
    lengths = jnp.asarray(profile(number_of, total, reach, slope), jnp.int32)
    twos = (number_of - 1) // 2
    source_of, taker = lengths[1:1 + 2 * twos:2], lengths[2:2 + 2 * twos:2]
    slack = jnp.minimum(source_of - 1, reach - taker)
    moved = jax.random.randint(jax.random.fold_in(rng, 1), (twos,), 0, 1 << 20) % (slack + 1)
    lengths = lengths.at[1:1 + 2 * twos:2].set(source_of - moved).at[2:2 + 2 * twos:2].set(taker + moved)
    return lengths[jax.random.permutation(jax.random.fold_in(rng, 2), number_of)]


def centred(rng, shape, deviation, reach, cuts=(), kind=jnp.bfloat16):
    gain = level_of(rng, shape, cuts, -0.22, 0.18) if cuts else 1.0
    values = jax.random.normal(rng, shape, jnp.float32) * deviation * gain
    return jnp.minimum(jnp.maximum(values, -reach), reach).astype(kind)


def setup_inputs(seed: int = 0, part: int = 0) -> dict:
    arg_keys = jax.random.split(jax.random.key(seed), 6)
    own_keys = jax.random.split(jax.random.fold_in(arg_keys[5], part), 6)
    return {
        "left_env": centred(own_keys[0], (SECTORS, B, B), 1.0, 6.0, ((0, 8), (1, 2))),
        "site_tensor": centred(own_keys[1], (SECTORS, PHYS, B, B), B ** -0.5, 0.1875, ((0, 8), (3, 2))),
        "left_sizes": uneven(own_keys[2], SECTORS, SECTORS * B // 2, B, 1).astype(jnp.int32),
        "right_sizes": uneven(own_keys[3], SECTORS, SECTORS * B // 2, B, 1).astype(jnp.int32),
        "targets": distinct(own_keys[4], SECTORS, SECTORS, PHYS, 8192),
    }


def reference(left_env, site_tensor, left_sizes, right_sizes, targets):
    sectors = left_env.shape[0]
    span = left_env.shape[1]
    rows = jnp.arange(span, dtype=jnp.int32)

    def one_sector(carry, index):
        block = left_env[index].astype(jnp.float32)
        tensors = site_tensor[index]
        reached = targets[index]
        live_cols = right_sizes[reached]
        keep = (rows[None, :, None] < left_sizes[index]) & (rows[None, None, :] < live_cols[:, None, None])
        masked = jnp.where(keep, tensors, jnp.zeros((), jnp.bfloat16)).astype(jnp.float32)
        product = jnp.einsum("ik,skj->sij", block, masked).astype(jnp.bfloat16)
        term = jnp.einsum("ski,skj->sij", masked, product.astype(jnp.float32)).astype(jnp.bfloat16)
        carry = carry.at[reached].add(term.astype(jnp.float32))
        return carry, None

    start = jnp.zeros((sectors, span, span), jnp.float32)
    result, unused = lax.scan(one_sector, start, jnp.arange(sectors, dtype=jnp.int32))
    return result
```

```python
import functools

import jax
import jax.numpy as jnp
from jax import lax
from jax.experimental import pallas as pl
from jax.experimental.pallas import tpu as pltpu
from jax.sharding import PartitionSpec as P

TILE = 256


def meta_kernel(sectors, states, width, left_ref, right_ref, target_ref, out_ref):
    def rank_sector(r, large):
        size = right_ref[r]

        def count(other, total):
            bigger = (right_ref[other] > size) | ((right_ref[other] == size) & (other < r))
            return total + bigger.astype(jnp.int32)

        rank = lax.fori_loop(0, sectors, count, jnp.int32(0))
        out_ref[0, r] = rank
        out_ref[1, rank] = size
        out_ref[2, rank] = jnp.int32(-1)
        out_ref[3, rank] = jnp.int32(0)
        out_ref[4, r] = jnp.int32(0)
        out_ref[5, r] = jnp.int32(0)
        return large + (size > width).astype(jnp.int32)

    large = lax.fori_loop(0, sectors, rank_sector, jnp.int32(0))
    for s in range(states):
        out_ref[2, out_ref[0, target_ref[0, s]]] = jnp.int32(s)

    def place(k, used):
        state = out_ref[2, k]
        wanted = (state >= 0) & (out_ref[1, k] > width)

        @pl.when(wanted)
        def _():
            out_ref[3, k] = used
            out_ref[4, used] = state

        return used + wanted.astype(jnp.int32)

    used = lax.fori_loop(0, sectors, place, jnp.int32(0))
    out_ref[5, 0] = left_ref[0]
    out_ref[5, 1] = used
    out_ref[5, 2] = large


def term_kernel(lo, hi, mode, states, span, width, splits, *refs):
    meta, t_hbm, own_hbm = refs[:3]
    others_e = refs[3 : 3 + splits - 1]
    at = 3 + splits - 1
    crossing = mode != "small"
    others_t = refs[at : at + (splits - 1) * states] if crossing else ()
    at += len(others_t)
    out_hbm, env, mine, theirs, product, result, env_sem, mine_sem, theirs_sem, out_sem = refs[at:]
    me = lax.axis_index("split")
    live_rows = meta[5, 0]
    blocks = (live_rows + TILE - 1) // TILE
    count = hi - lo

    def env_copies():
        copies = [pltpu.make_async_copy(own_hbm, env.at[pl.ds(pl.multiple_of(me * width, width), width)], env_sem.at[0])]
        for h in range(1, splits):
            source = lax.rem(me - h + splits, splits)
            copies.append(
                pltpu.make_async_copy(
                    others_e[h - 1], env.at[pl.ds(pl.multiple_of(source * width, width), width)], env_sem.at[h]
                )
            )
        return copies

    for copy in env_copies():
        copy.start()

    def wanted(k):
        size = meta[1, k]
        yes = (meta[2, k] >= 0) & (size > me * width)
        if mode == "small":
            yes = yes & (size <= width)
        if mode == "large":
            yes = yes & (size > width)
        return yes

    def mine_copy(k, i):
        return pltpu.make_async_copy(t_hbm.at[meta[2, k]], mine.at[i % 2], mine_sem.at[i % 2])

    def theirs_start(k, i):
        for slot in range(states):
            @pl.when(meta[3, k] == slot)
            def _():
                for h in range(1, splits):
                    pltpu.make_async_copy(
                        others_t[(h - 1) * states + slot], theirs.at[i % 2, h - 1], theirs_sem.at[i % 2, h - 1]
                    ).start()

    def theirs_wait(i):
        for h in range(1, splits):
            pltpu.make_async_copy(others_t[(h - 1) * states], theirs.at[i % 2, h - 1], theirs_sem.at[i % 2, h - 1]).wait()

    def begin(k, i):
        @pl.when(wanted(k))
        def _():
            mine_copy(k, i).start()

        if crossing:
            @pl.when(wanted(k) & (meta[1, k] > width))
            def _():
                theirs_start(k, i)

    def out_copy(i):
        return pltpu.make_async_copy(result.at[i], out_hbm.at[i], out_sem.at[i])

    begin(lo, 0)
    for copy in env_copies():
        copy.wait()

    def mask(ref, cols):
        def step(b, carry):
            base = pl.multiple_of(b * TILE, TILE)
            rows_here = lax.broadcasted_iota(jnp.int32, (TILE, width), 0) + base
            cols_here = lax.broadcasted_iota(jnp.int32, (TILE, width), 1)
            keep = (rows_here < live_rows) & (cols_here < cols)
            ref[pl.ds(base, TILE), :] = jnp.where(keep, ref[pl.ds(base, TILE), :], jnp.zeros((), jnp.bfloat16))
            return carry

        lax.fori_loop(0, blocks, step, 0)

    def half(i, ref, depth, row_base):
        def step(j, carry):
            base = pl.multiple_of(j * TILE, TILE)
            value = lax.dot_general(
                ref[:depth, pl.ds(base, TILE)], product[:depth, :], (((0,), (0,)), ((), ())),
                preferred_element_type=jnp.float32,
            )
            result[i, pl.ds(pl.multiple_of(row_base + base, TILE), TILE), :] = value.astype(jnp.bfloat16)
            return carry

        lax.fori_loop(0, width // TILE, step, 0)

    def one(i, carry):
        k = lo + i
        size = meta[1, k]

        @pl.when(i + 1 < count)
        def _():
            begin(k + 1, i + 1)

        @pl.when(jnp.logical_not(wanted(k)))
        def _():
            result[i] = jnp.zeros((span, width), jnp.bfloat16)

        @pl.when(wanted(k))
        def _():
            mine_copy(k, i).wait()
            mask(mine.at[i % 2], size - me * width)

            def multiply(depth):
                def step(b, carry):
                    base = pl.multiple_of(b * TILE, TILE)
                    value = jnp.dot(
                        env[pl.ds(base, TILE), :depth], mine[i % 2, :depth, :], preferred_element_type=jnp.float32
                    )
                    product[pl.ds(base, TILE), :] = value.astype(jnp.bfloat16)
                    return carry

                lax.fori_loop(0, depth // TILE, step, 0)
                half(i, mine.at[i % 2], depth, me * width)

            for v in range(1, span // TILE + 1):
                @pl.when(blocks == v)
                def _():
                    multiply(v * TILE)

            if not crossing:
                for h in range(1, splits):
                    base = pl.multiple_of(lax.rem(me - h + splits, splits) * width, width)
                    result[i, pl.ds(base, width), :] = jnp.zeros((width, width), jnp.bfloat16)
            else:
                @pl.when(size > width)
                def _():
                    theirs_wait(i)

                for h in range(1, splits):
                    source = lax.rem(me - h + splits, splits)
                    base = pl.multiple_of(source * width, width)
                    some = size > source * width

                    @pl.when(jnp.logical_not((size > width) & some))
                    def _():
                        result[i, pl.ds(base, width), :] = jnp.zeros((width, width), jnp.bfloat16)

                    @pl.when((size > width) & some)
                    def _():
                        mask(theirs.at[i % 2, h - 1], size - source * width)
                        for v in range(1, span // TILE + 1):
                            @pl.when(blocks == v)
                            def _():
                                half(i, theirs.at[i % 2, h - 1], v * TILE, base)

        out_copy(i).start()
        return carry

    lax.fori_loop(0, count, one, 0)
    lax.fori_loop(0, count, lambda i, carry: (out_copy(i).wait(), carry)[1], 0)


def terms(lo, hi, mode, meta, tensor, env, other_env, other_tensor, splits):
    states, span, width = tensor.shape
    crossing = mode != "small"
    extra = list(other_tensor) if crossing else []
    kernel = functools.partial(term_kernel, lo, hi, mode, states, span, width, splits)
    count = hi - lo
    return pl.pallas_call(
        kernel,
        out_shape=jax.ShapeDtypeStruct((count, span, width), jnp.bfloat16),
        in_specs=[pl.BlockSpec(memory_space=pltpu.SMEM)]
        + [pl.BlockSpec(memory_space=pl.ANY)] * (2 + len(other_env) + len(extra)),
        out_specs=pl.BlockSpec(memory_space=pl.ANY),
        scratch_shapes=[
            pltpu.VMEM((span, span), jnp.bfloat16),
            pltpu.VMEM((2, span, width), jnp.bfloat16),
            pltpu.VMEM((2, max(splits - 1, 1), span, width) if crossing else (1, 1, 16, 128), jnp.bfloat16),
            pltpu.VMEM((span, width), jnp.bfloat16),
            pltpu.VMEM((count, span, width), jnp.bfloat16),
            pltpu.SemaphoreType.DMA((splits,)),
            pltpu.SemaphoreType.DMA((2,)),
            pltpu.SemaphoreType.DMA((2, max(splits - 1, 1))),
            pltpu.SemaphoreType.DMA((count,)),
        ],
        compiler_params=pltpu.CompilerParams(vmem_limit_bytes=48 * 1024 * 1024),
    )(meta, tensor, env, *other_env, *extra)


def finish_kernel(sectors, lead, meta, large_ref, small_ref, out_ref):
    for r in range(sectors):
        rank = meta[0, r]

        @pl.when(rank < lead)
        def _():
            out_ref[r] = large_ref[jnp.minimum(rank, lead - 1)].astype(jnp.float32)

        @pl.when(rank >= lead)
        def _():
            out_ref[r] = small_ref[jnp.maximum(rank - lead, 0)].astype(jnp.float32)


def body(left_env, site_tensor, left_sizes, right_sizes, targets):
    splits = lax.axis_size("split")
    tensor = site_tensor[0]
    env = left_env[0]
    states, span, width = tensor.shape
    sectors = right_sizes.shape[0]
    lead = sectors // 2
    smem = pl.BlockSpec(memory_space=pltpu.SMEM)

    meta = pl.pallas_call(
        functools.partial(meta_kernel, sectors, states, width),
        out_shape=jax.ShapeDtypeStruct((6, max(sectors, 8)), jnp.int32),
        in_specs=[smem] * 3,
        out_specs=smem,
    )(left_sizes, right_sizes, targets)

    shifts = [[(y, (y + h) % splits) for y in range(splits)] for h in range(1, splits)]
    depths = max(span // TILE // (splits - 1), 1) if splits > 1 else 1
    grain = span // depths
    blocks = (left_sizes[0] + grain - 1) // grain

    def send_env(v):
        rows = min(v * grain, width)
        senders = -(-v * grain // width)

        def branch(block):
            piece = block[:rows, : v * grain]
            got = [lax.ppermute(piece, "split", [p for p in pairs if p[0] < senders]) for pairs in shifts]
            return tuple(jnp.pad(g, ((0, width - rows), (0, span - v * grain))) for g in got)

        return branch

    other_env = lax.switch(blocks - 1, [send_env(v) for v in range(1, depths + 1)], env)

    small = terms(lead, sectors, "small", meta, tensor, env, other_env, (), splits)
    small, tensor = lax.optimization_barrier((small, tensor))
    small_sum = lax.psum_scatter(small, "charge", scatter_dimension=1, tiled=True)

    def send_tensor(used, v):
        def branch(block, slots):
            zero = jnp.zeros((span, width), jnp.bfloat16)
            got = []
            for pairs in shifts:
                for i in range(states):
                    if i >= used:
                        got.append(zero)
                        continue
                    piece = lax.dynamic_slice(block, (slots[i], 0, 0), (1, v * grain, width))[0]
                    got.append(jnp.pad(lax.ppermute(piece, "split", pairs), ((0, span - v * grain), (0, 0))))
            return tuple(got)

        return branch

    used = meta[5, 1]
    index = jnp.where(used == 0, 0, 1 + (used - 1) * depths + blocks - 1)
    branches = [send_tensor(0, 1)] + [send_tensor(u, v) for u in range(1, states + 1) for v in range(1, depths + 1)]
    other_tensor = lax.switch(index, branches, tensor, meta[4, :states])

    large = terms(0, lead, "all", meta, tensor, env, other_env, other_tensor, splits)
    large_sum = lax.psum_scatter(large, "charge", scatter_dimension=1, tiled=True)

    most = meta[5, 2]
    groups = lax.axis_size("groups")
    for h in range(1, groups):
        sizes = lax.ppermute(right_sizes, "groups", [(g, (g + h) % groups) for g in range(groups)])
        most = jnp.maximum(most, jnp.sum((sizes > width).astype(jnp.int32)))

    def rest(total):
        more = terms(lead, sectors, "large", meta, tensor, env, other_env, other_tensor, splits)
        return total + lax.psum_scatter(more, "charge", scatter_dimension=1, tiled=True)

    small_sum = lax.cond(most > lead, rest, lambda total: total, small_sum)

    rows = large_sum.shape[1]
    vmem = pl.BlockSpec(memory_space=pltpu.VMEM)
    return pl.pallas_call(
        functools.partial(finish_kernel, sectors, lead),
        out_shape=jax.ShapeDtypeStruct((sectors, rows, width), jnp.float32),
        in_specs=[smem, vmem, vmem],
        out_specs=vmem,
        compiler_params=pltpu.CompilerParams(vmem_limit_bytes=48 * 1024 * 1024),
    )(meta, large_sum, small_sum)


def solution(mesh):
    in_specs = (
        P(("groups", "charge"), "split", None),
        P(("groups", "charge"), None, None, "split"),
        P(("groups", "charge")),
        P("groups"),
        P(("groups", "charge"), None),
    )
    out_specs = P("groups", "charge", "split")
    return jax.shard_map(body, mesh=mesh, in_specs=in_specs, out_specs=out_specs, check_vma=False)
```

```python
import functools

import jax
import jax.numpy as jnp
from jax import lax
from jax.experimental import pallas as pl
from jax.experimental.pallas import tpu as pltpu
from jax.sharding import PartitionSpec as P

TILE = 256


def meta_kernel(sectors, states, width, left_ref, right_ref, target_ref, out_ref):
    def rank_sector(r, large):
        size = right_ref[r]

        def count(other, total):
            bigger = (right_ref[other] > size) | ((right_ref[other] == size) & (other < r))
            return total + bigger.astype(jnp.int32)

        rank = lax.fori_loop(0, sectors, count, jnp.int32(0))
        out_ref[0, r] = rank
        out_ref[1, rank] = size
        out_ref[2, rank] = jnp.int32(-1)
        out_ref[3, rank] = jnp.int32(0)
        out_ref[4, r] = jnp.int32(0)
        out_ref[5, r] = jnp.int32(0)
        return large + (size > width).astype(jnp.int32)

    large = lax.fori_loop(0, sectors, rank_sector, jnp.int32(0))
    for s in range(states):
        out_ref[2, out_ref[0, target_ref[0, s]]] = jnp.int32(s)

    def place(k, used):
        state = out_ref[2, k]
        wanted = (state >= 0) & (out_ref[1, k] > width)

        @pl.when(wanted)
        def _():
            out_ref[3, k] = used
            out_ref[4, used] = state

        return used + wanted.astype(jnp.int32)

    used = lax.fori_loop(0, sectors, place, jnp.int32(0))
    out_ref[5, 0] = left_ref[0]
    out_ref[5, 1] = used
    out_ref[5, 2] = large


def own_kernel(lo, hi, keep, step_rows, states, span, width, splits, *refs):
    meta, t_hbm, own_hbm = refs[:3]
    others_e = refs[3 : 3 + splits - 1]
    at = 3 + splits - 1
    out_hbm = refs[at]
    products_hbm = refs[at + 1] if keep else None
    env, mine, product, result, env_sem, mine_sem, out_sem, product_sem = refs[at + 1 + int(keep) :]
    me = lax.axis_index("split")
    live_rows = meta[5, 0]
    reach = (live_rows + step_rows - 1) // step_rows
    count = hi - lo

    def source_base(h):
        return pl.multiple_of(lax.rem(me - h + splits, splits) * width, width)

    env_copies = [pltpu.make_async_copy(own_hbm, env.at[pl.ds(source_base(0), width)], env_sem.at[0])] + [
        pltpu.make_async_copy(others_e[h - 1], env.at[pl.ds(source_base(h), width)], env_sem.at[h])
        for h in range(1, splits)
    ]

    def wanted(k):
        return (meta[2, k] >= 0) & (meta[1, k] > me * width)

    def crossing(k):
        return wanted(k) & (meta[1, k] > width)

    def mine_copy(k, i):
        return pltpu.make_async_copy(t_hbm.at[meta[2, k]], mine.at[i % 2], mine_sem.at[i % 2])

    def begin(k, i):
        @pl.when(wanted(k))
        def _():
            mine_copy(k, i).start()

    def out_copy(i):
        return pltpu.make_async_copy(result.at[i], out_hbm.at[i], out_sem.at[i])

    def product_copy(i):
        return pltpu.make_async_copy(product.at[i], products_hbm.at[i], product_sem.at[i])

    for copy in env_copies:
        copy.start()
    begin(lo, 0)
    for copy in env_copies:
        copy.wait()

    def one(i, carry):
        k = lo + i
        size = meta[1, k]
        p = i if keep else 0

        @pl.when(i + 1 < count)
        def _():
            begin(k + 1, i + 1)

        @pl.when(jnp.logical_not(wanted(k)))
        def _():
            result[i] = jnp.zeros((span, width), jnp.bfloat16)

        @pl.when(wanted(k))
        def _():
            mine_copy(k, i).wait()
            mask(mine.at[i % 2], size - me * width, live_rows, reach * (step_rows // TILE), width)

            def multiply(depth):
                def step(b, carry):
                    base = pl.multiple_of(b * TILE, TILE)
                    value = jnp.dot(
                        env[pl.ds(base, TILE), :depth], mine[i % 2, :depth, :], preferred_element_type=jnp.float32
                    )
                    product[p, pl.ds(base, TILE), :] = value.astype(jnp.bfloat16)
                    return carry

                lax.fori_loop(0, depth // TILE, step, 0)
                half(result.at[i], mine.at[i % 2], product.at[p], depth, me * width, width)

            for v in range(1, span // step_rows + 1):
                @pl.when(reach == v)
                def _():
                    multiply(v * step_rows)

            for h in range(1, splits):
                @pl.when(jnp.logical_not((size > width) & (size > source_base(h))))
                def _():
                    result[i, pl.ds(source_base(h), width), :] = jnp.zeros((width, width), jnp.bfloat16)

        out_copy(i).start()
        if keep:
            @pl.when(crossing(k))
            def _():
                product_copy(i).start()
        return carry

    lax.fori_loop(0, count, one, 0)

    def finish(i, carry):
        out_copy(i).wait()
        if keep:
            @pl.when(crossing(lo + i))
            def _():
                product_copy(i).wait()
        return carry

    lax.fori_loop(0, count, finish, 0)


def mask(ref, cols, live_rows, tiles, width):
    def step(b, carry):
        base = pl.multiple_of(b * TILE, TILE)
        rows_here = lax.broadcasted_iota(jnp.int32, (TILE, width), 0) + base
        cols_here = lax.broadcasted_iota(jnp.int32, (TILE, width), 1)
        keep = (rows_here < live_rows) & (cols_here < cols)
        ref[pl.ds(base, TILE), :] = jnp.where(keep, ref[pl.ds(base, TILE), :], jnp.zeros((), jnp.bfloat16))
        return carry

    lax.fori_loop(0, tiles, step, 0)


def half(result, factor, product, depth, row_base, width):
    def step(j, carry):
        base = pl.multiple_of(j * TILE, TILE)
        value = lax.dot_general(
            factor[:depth, pl.ds(base, TILE)], product[:depth, :], (((0,), (0,)), ((), ())),
            preferred_element_type=jnp.float32,
        )
        result[pl.ds(pl.multiple_of(row_base + base, TILE), TILE), :] = value.astype(jnp.bfloat16)
        return carry

    lax.fori_loop(0, width // TILE, step, 0)


def other_kernel(count, states, span, width, splits, *refs):
    meta, products_hbm = refs[0], refs[2]
    others_t = refs[3 : 3 + (splits - 1) * states]
    out_hbm, theirs, product, result, theirs_sem, product_sem, out_sem = refs[3 + len(others_t) :]
    me = lax.axis_index("split")
    live_rows = meta[5, 0]
    blocks = (live_rows + TILE - 1) // TILE

    def source_base(h):
        return pl.multiple_of(lax.rem(me - h + splits, splits) * width, width)

    def wanted(k, h):
        size = meta[1, k]
        return (meta[2, k] >= 0) & (size > me * width) & (size > width) & (size > source_base(h))

    def product_copy(k):
        return pltpu.make_async_copy(products_hbm.at[k], product.at[k % 2], product_sem.at[k % 2])

    def theirs_copy(k, h, slot):
        return pltpu.make_async_copy(others_t[(h - 1) * states + slot], theirs.at[k % 2, h - 1], theirs_sem.at[k % 2, h - 1])

    def out_copy(k, h):
        return pltpu.make_async_copy(
            result.at[k, h - 1], out_hbm.at[k, pl.ds(source_base(h), width)], out_sem.at[k, h - 1]
        )

    def crossing(k):
        return (meta[2, k] >= 0) & (meta[1, k] > me * width) & (meta[1, k] > width)

    def begin(k):
        @pl.when(crossing(k))
        def _():
            product_copy(k).start()
            for slot in range(states):
                @pl.when(meta[3, k] == slot)
                def _():
                    for h in range(1, splits):
                        theirs_copy(k, h, slot).start()

    begin(0)

    def one(k, carry):
        @pl.when(k + 1 < count)
        def _():
            begin(k + 1)

        @pl.when(crossing(k))
        def _():
            product_copy(k).wait()
            for h in range(1, splits):
                theirs_copy(k, h, 0).wait()
            for h in range(1, splits):
                @pl.when(wanted(k, h))
                def _():
                    mask(theirs.at[k % 2, h - 1], meta[1, k] - source_base(h), live_rows, blocks, width)
                    for v in range(1, span // TILE + 1):
                        @pl.when(blocks == v)
                        def _():
                            half(result.at[k, h - 1], theirs.at[k % 2, h - 1], product.at[k % 2], v * TILE, 0, width)
                    out_copy(k, h).start()

        return carry

    lax.fori_loop(0, count, one, 0)

    def finish(k, carry):
        for h in range(1, splits):
            @pl.when(wanted(k, h))
            def _():
                out_copy(k, h).wait()
        return carry

    lax.fori_loop(0, count, finish, 0)


ANY = pl.BlockSpec(memory_space=pl.ANY)
HBM = pl.BlockSpec(memory_space=pltpu.HBM)
SMEM = pl.BlockSpec(memory_space=pltpu.SMEM)
PARAMS = pltpu.CompilerParams(vmem_limit_bytes=48 * 1024 * 1024)


def own_terms(lo, hi, keep, meta, tensor, env, other_env, splits):
    states, span, width = tensor.shape
    count = hi - lo
    block = jax.ShapeDtypeStruct((count, span, width), jnp.bfloat16)
    return pl.pallas_call(
        functools.partial(own_kernel, lo, hi, keep, max(TILE, span // 2) if keep else TILE, states, span, width, splits),
        out_shape=[block, block] if keep else [block],
        in_specs=[SMEM] + [ANY] * (2 + len(other_env)),
        out_specs=[HBM, HBM] if keep else [HBM],
        scratch_shapes=[
            pltpu.VMEM((span, span), jnp.bfloat16),
            pltpu.VMEM((2, span, width), jnp.bfloat16),
            pltpu.VMEM((count if keep else 1, span, width), jnp.bfloat16),
            pltpu.VMEM((count, span, width), jnp.bfloat16),
            pltpu.SemaphoreType.DMA((splits,)),
            pltpu.SemaphoreType.DMA((2,)),
            pltpu.SemaphoreType.DMA((count,)),
            pltpu.SemaphoreType.DMA((count,)),
        ],
        compiler_params=PARAMS,
        cost_estimate=pl.CostEstimate(
            flops=4 * states * span * span * width, bytes_accessed=4 * count * span * width, transcendentals=0
        ),
    )(meta, tensor, env, *other_env)


def other_terms(meta, result, products, other_tensor, states, splits):
    count, span, width = result.shape
    return pl.pallas_call(
        functools.partial(other_kernel, count, states, span, width, splits),
        out_shape=jax.ShapeDtypeStruct(result.shape, jnp.bfloat16),
        in_specs=[SMEM, HBM, ANY] + [ANY] * len(other_tensor),
        out_specs=HBM,
        input_output_aliases={1: 0},
        scratch_shapes=[
            pltpu.VMEM((2, max(splits - 1, 1), span, width), jnp.bfloat16),
            pltpu.VMEM((2, span, width), jnp.bfloat16),
            pltpu.VMEM((count, max(splits - 1, 1), width, width), jnp.bfloat16),
            pltpu.SemaphoreType.DMA((2, max(splits - 1, 1))),
            pltpu.SemaphoreType.DMA((2,)),
            pltpu.SemaphoreType.DMA((count, max(splits - 1, 1))),
        ],
        compiler_params=PARAMS,
    )(meta, result, products, *other_tensor)


def finish_kernel(sectors, lead, meta, large_ref, *refs):
    out_ref = refs[-1]
    for r in range(sectors):
        rank = meta[0, r]

        @pl.when(rank < lead)
        def _():
            out_ref[r] = large_ref[jnp.minimum(rank, lead - 1)].astype(jnp.float32)

        if lead < sectors:
            @pl.when(rank >= lead)
            def _():
                out_ref[r] = refs[0][jnp.maximum(rank - lead, 0)].astype(jnp.float32)


def body(left_env, site_tensor, left_sizes, right_sizes, targets):
    splits = lax.axis_size("split")
    groups = lax.axis_size("groups")
    states, span, width = site_tensor.shape[1:]
    sectors = right_sizes.shape[0]

    most = jnp.sum((right_sizes > width).astype(jnp.int32))
    for h in range(1, groups):
        sizes = lax.ppermute(right_sizes, "groups", [(g, (g + h) % groups) for g in range(groups)])
        most = jnp.maximum(most, jnp.sum((sizes > width).astype(jnp.int32)))

    meta = pl.pallas_call(
        functools.partial(meta_kernel, sectors, states, width),
        out_shape=jax.ShapeDtypeStruct((6, max(sectors, 8)), jnp.int32),
        in_specs=[SMEM] * 3,
        out_specs=SMEM,
    )(left_sizes, right_sizes, targets)

    shifts = [[(y, (y + h) % splits) for y in range(splits)] for h in range(1, splits)]
    depths = max(span // TILE // (splits - 1), 1) if splits > 1 else 1
    grain = span // depths
    blocks = (left_sizes[0] + grain - 1) // grain

    def send_env(v):
        rows = min(v * grain, width)
        senders = -(-v * grain // width)

        def branch(block):
            piece = block[:rows, : v * grain]
            got = [lax.ppermute(piece, "split", [p for p in pairs if p[0] < senders]) for pairs in shifts]
            return tuple(jnp.pad(g, ((0, width - rows), (0, span - v * grain))) for g in got)

        return branch

    other_env = lax.switch(blocks - 1, [send_env(v) for v in range(1, depths + 1)], left_env[0])

    used = meta[5, 1]
    exchange = jnp.where(used == 0, 0, 1 + (used - 1) * depths + blocks - 1)

    def send_tensor(lead, used, v):
        def branch(block, env, other_env, meta):
            zero = jnp.zeros((span, width), jnp.bfloat16)
            got = []
            for pairs in shifts:
                for i in range(states):
                    if i >= used:
                        got.append(zero)
                        continue
                    piece = lax.dynamic_slice(block, (meta[4, i], 0, 0), (1, v * grain, width))[0]
                    got.append(jnp.pad(lax.ppermute(piece, "split", pairs), ((0, span - v * grain), (0, 0))))
            result, products = own_terms(0, lead, True, meta, block, env, other_env, splits)
            return result, products, tuple(got)

        return branch

    def run(lead):
        def branch(env, tensor, other_env, meta, index):
            sums = []
            if lead < sectors:
                (small,) = own_terms(lead, sectors, False, meta, tensor, env, other_env, splits)
                small, tensor = lax.optimization_barrier((small, tensor))
                sums = [lax.psum_scatter(small, "charge", scatter_dimension=1, tiled=True)]
            if lead < sectors:
                branches = [send_tensor(lead, 0, 1)] + [
                    send_tensor(lead, u, v) for u in range(1, min(states, lead) + 1) for v in range(1, depths + 1)
                ]
                result, products, other_tensor = lax.switch(index, branches, tensor, env, other_env, meta)
            else:
                result, products, other_tensor = send_tensor(lead, states, depths)(tensor, env, other_env, meta)
            large = other_terms(meta, result, products, other_tensor, states, splits)
            sums = [lax.psum_scatter(large, "charge", scatter_dimension=1, tiled=True)] + sums
            vmem = pl.BlockSpec(memory_space=pltpu.VMEM)
            return pl.pallas_call(
                functools.partial(finish_kernel, sectors, lead),
                out_shape=jax.ShapeDtypeStruct((sectors, sums[0].shape[1], width), jnp.float32),
                in_specs=[SMEM] + [vmem] * len(sums),
                out_specs=vmem,
                compiler_params=PARAMS,
            )(meta, *sums)

        return branch

    leads = sorted({max(sectors * e // 8, 1) for e in (3, 4, 5, 8)})
    choice = sum((most > lead).astype(jnp.int32) for lead in leads[:-1])
    return lax.switch(choice, [run(lead) for lead in leads], left_env[0], site_tensor[0], other_env, meta, exchange)


def solution(mesh):
    in_specs = (
        P(("groups", "charge"), "split", None),
        P(("groups", "charge"), None, None, "split"),
        P(("groups", "charge")),
        P("groups"),
        P(("groups", "charge"), None),
    )
    out_specs = P("groups", "charge", "split")
    return jax.shard_map(body, mesh=mesh, in_specs=in_specs, out_specs=out_specs, check_vma=False)
```

```python
import functools

import jax
import jax.numpy as jnp
from jax import lax
from jax.experimental import pallas as pl
from jax.experimental.pallas import tpu as pltpu
from jax.sharding import PartitionSpec as P

TILE = 256


def meta_kernel(sectors, states, width, depths, grain, leads, left_ref, target_ref, right_ref, *refs):
    others, out_ref = refs[:-1], refs[-1]

    def rank_sector(r, carry):
        size = right_ref[r]

        def count(other, total):
            bigger = (right_ref[other] > size) | ((right_ref[other] == size) & (other < r))
            return total + bigger.astype(jnp.int32)

        rank = lax.fori_loop(0, sectors, count, jnp.int32(0), unroll=True)
        out_ref[0, r] = rank
        out_ref[1, rank] = size
        out_ref[2, rank] = jnp.int32(-1)
        out_ref[3, rank] = jnp.int32(states)
        out_ref[4, r] = jnp.int32(0)
        out_ref[5, r] = jnp.int32(0)
        return carry

    lax.fori_loop(0, sectors, rank_sector, 0)
    for s in range(states):
        out_ref[2, out_ref[0, target_ref[0, s]]] = jnp.int32(s)

    def place(k, used):
        state = out_ref[2, k]
        wanted = (state >= 0) & (out_ref[1, k] > width)

        @pl.when(wanted)
        def _():
            out_ref[3, k] = used
            out_ref[4, used] = state

        return used + wanted.astype(jnp.int32)

    used = lax.fori_loop(0, sectors, place, jnp.int32(0))
    most = jnp.int32(0)
    for ref in (right_ref,) + others:
        def wide(r, total, ref=ref):
            return total + (ref[r] > width).astype(jnp.int32)

        most = jnp.maximum(most, lax.fori_loop(0, sectors, wide, jnp.int32(0)))
    lead, choice = jnp.int32(leads[-1]), jnp.int32(0)
    for e in reversed(leads[:-1]):
        lead = jnp.where(most <= e, jnp.int32(e), lead)
    for e in leads[:-1]:
        choice = choice + (most > e).astype(jnp.int32)
    depth = (left_ref[0] + grain - 1) // grain
    out_ref[5, 0] = left_ref[0]
    out_ref[5, 1] = lead
    out_ref[5, 2] = choice
    out_ref[5, 3] = jnp.where(used <= 1, 0, 1 + (used - 2) * depths + depth - 1)


def own_kernel(first, sectors, wide, states, span, width, splits, *refs):
    meta, t_hbm, own_hbm = refs[:3]
    others_e = refs[3 : 3 + splits - 1]
    at = 3 + splits - 1
    out_hbm = refs[at]
    products_hbm = refs[at + 1] if wide else None
    env, mine, product, result, env_sem, mine_sem, out_sem, product_sem = refs[at + 1 + int(wide) :]
    me = lax.axis_index("split")
    live_rows = meta[5, 0]
    tiles = (live_rows + TILE - 1) // TILE
    start = 0 if wide else first
    stop = meta[5, 1] if wide else sectors

    def source_base(h):
        return pl.multiple_of(lax.rem(me - h + splits, splits) * width, width)

    env_copies = [pltpu.make_async_copy(own_hbm, env.at[pl.ds(source_base(0), width)], env_sem.at[0])] + [
        pltpu.make_async_copy(others_e[h - 1], env.at[pl.ds(source_base(h), width)], env_sem.at[h])
        for h in range(1, splits)
    ]

    def wanted(k):
        yes = (meta[2, k] >= 0) & (meta[1, k] > me * width)
        if wide:
            return yes & ((k < first) | (meta[1, k] > width))
        return yes & (meta[1, k] <= width)

    def crossing(k):
        return wanted(k) & (meta[1, k] > width)

    def mine_copy(k):
        return pltpu.make_async_copy(t_hbm.at[meta[2, k]], mine.at[k % 2], mine_sem.at[k % 2])

    def begin(k):
        @pl.when(wanted(k))
        def _():
            mine_copy(k).start()

    def out_copy(k):
        return pltpu.make_async_copy(result.at[k - start], out_hbm.at[k - start], out_sem.at[k - start])

    def product_copy(k):
        return pltpu.make_async_copy(product.at[meta[3, k]], products_hbm.at[meta[3, k]], product_sem.at[meta[3, k]])

    for copy in env_copies:
        copy.start()
    begin(start)
    for copy in env_copies:
        copy.wait()

    def one(k, carry):
        size = meta[1, k]
        p = meta[3, k] if wide else 0
        i = k - start

        @pl.when(k + 1 < stop)
        def _():
            begin(k + 1)

        @pl.when(jnp.logical_not(wanted(k)))
        def _():
            result[i] = jnp.zeros(result.shape[1:], jnp.bfloat16)

        @pl.when(wanted(k))
        def _():
            mine_copy(k).wait()
            mask(mine.at[k % 2], size - me * width, live_rows, width)

            def multiply(b, carry):
                base = pl.multiple_of(b * TILE, TILE)
                value = jnp.dot(env[pl.ds(base, TILE), :], mine[k % 2], preferred_element_type=jnp.float32)
                product[p, pl.ds(base, TILE), :] = value.astype(jnp.bfloat16)
                return carry

            def clear(b, carry):
                product[p, pl.ds(pl.multiple_of(b * TILE, TILE), TILE), :] = jnp.zeros((TILE, width), jnp.bfloat16)
                return carry

            lax.fori_loop(0, tiles, multiply, 0)
            lax.fori_loop(tiles, span // TILE, clear, 0)
            half(result.at[i], mine.at[k % 2], product.at[p], me * width if wide else 0, width)
            if wide:
                for h in range(1, splits):
                    @pl.when(jnp.logical_not((size > width) & (size > source_base(h))))
                    def _():
                        result[i, pl.ds(source_base(h), width), :] = jnp.zeros((width, width), jnp.bfloat16)

        out_copy(k).start()
        if wide:
            @pl.when(crossing(k))
            def _():
                product_copy(k).start()
        return carry

    lax.fori_loop(start, stop, one, 0)

    def finish(k, carry):
        out_copy(k).wait()
        if wide:
            @pl.when(crossing(k))
            def _():
                product_copy(k).wait()
        return carry

    lax.fori_loop(start, stop, finish, 0)


def mask(ref, cols, live_rows, width):
    def step(b, carry):
        base = pl.multiple_of(b * TILE, TILE)
        rows_here = lax.broadcasted_iota(jnp.int32, (TILE, width), 0) + base
        cols_here = lax.broadcasted_iota(jnp.int32, (TILE, width), 1)
        keep = (rows_here < live_rows) & (cols_here < cols)
        ref[pl.ds(base, TILE), :] = jnp.where(keep, ref[pl.ds(base, TILE), :], jnp.zeros((), jnp.bfloat16))
        return carry

    lax.fori_loop(0, ref.shape[0] // TILE, step, 0)


def half(result, factor, product, row_base, width):
    def step(j, carry):
        base = pl.multiple_of(j * TILE, TILE)
        value = lax.dot_general(
            factor[:, pl.ds(base, TILE)], product[...], (((0,), (0,)), ((), ())), preferred_element_type=jnp.float32
        )
        result[pl.ds(pl.multiple_of(row_base + base, TILE), TILE), :] = value.astype(jnp.bfloat16)
        return carry

    lax.fori_loop(0, width // TILE, step, 0)


def other_kernel(states, span, width, splits, *refs):
    meta, products_hbm = refs[0], refs[2]
    others_t = refs[3 : 3 + (splits - 1) * states]
    out_hbm, theirs, product, result, theirs_sem, product_sem, out_sem = refs[3 + len(others_t) :]
    me = lax.axis_index("split")
    live_rows = meta[5, 0]
    stop = meta[5, 1]

    def source_base(h):
        return pl.multiple_of(lax.rem(me - h + splits, splits) * width, width)

    def crossing(k):
        return (meta[2, k] >= 0) & (meta[1, k] > me * width) & (meta[1, k] > width)

    def wanted(k, h):
        return crossing(k) & (meta[1, k] > source_base(h))

    def product_copy(k):
        return pltpu.make_async_copy(products_hbm.at[meta[3, k]], product.at[k % 2], product_sem.at[k % 2])

    def theirs_copy(k, h, slot):
        return pltpu.make_async_copy(others_t[(h - 1) * states + slot], theirs.at[k % 2, h - 1], theirs_sem.at[k % 2, h - 1])

    def out_copy(k, h):
        return pltpu.make_async_copy(
            result.at[k, h - 1], out_hbm.at[k, pl.ds(source_base(h), width)], out_sem.at[k, h - 1]
        )

    def begin(k):
        @pl.when(crossing(k))
        def _():
            product_copy(k).start()
            for slot in range(states):
                @pl.when(meta[3, k] == slot)
                def _():
                    for h in range(1, splits):
                        theirs_copy(k, h, slot).start()

    begin(0)

    def one(k, carry):
        @pl.when(k + 1 < stop)
        def _():
            begin(k + 1)

        @pl.when(crossing(k))
        def _():
            product_copy(k).wait()
            for h in range(1, splits):
                theirs_copy(k, h, 0).wait()
            for h in range(1, splits):
                @pl.when(wanted(k, h))
                def _():
                    mask(theirs.at[k % 2, h - 1], meta[1, k] - source_base(h), live_rows, width)
                    half(result.at[k, h - 1], theirs.at[k % 2, h - 1], product.at[k % 2], 0, width)
                    out_copy(k, h).start()

        return carry

    lax.fori_loop(0, stop, one, 0)

    def finish(k, carry):
        for h in range(1, splits):
            @pl.when(wanted(k, h))
            def _():
                out_copy(k, h).wait()
        return carry

    lax.fori_loop(0, stop, finish, 0)


def finish_kernel(sectors, first, lead, width, pieces, meta, large_ref, *refs):
    small, out_ref = refs[:pieces], refs[pieces]
    rows = out_ref.shape[1] // pieces
    for r in range(sectors):
        rank = meta[0, r]
        in_second = (rank < first) | (meta[1, rank] > width)

        @pl.when(in_second)
        def _():
            out_ref[r] = large_ref[jnp.minimum(rank, lead - 1)].astype(jnp.float32)

        @pl.when(jnp.logical_not(in_second))
        def _():
            for p in range(pieces):
                out_ref[r, p * rows : (p + 1) * rows, :] = small[p][jnp.maximum(rank - first, 0)].astype(jnp.float32)


def blank_kernel(out_ref):
    pass


ANY = pl.BlockSpec(memory_space=pl.ANY)
HBM = pl.BlockSpec(memory_space=pltpu.HBM)
SMEM = pl.BlockSpec(memory_space=pltpu.SMEM)
VMEM = pl.BlockSpec(memory_space=pltpu.VMEM)
PARAMS = pltpu.CompilerParams(vmem_limit_bytes=62 * 1024 * 1024)


def own_terms(first, sectors, wide, meta, tensor, env, other_env, splits):
    states, span, width = tensor.shape
    count, rows = (sectors, span) if wide else (sectors - first, width)
    slots = states + 1 if wide else 1
    block = jax.ShapeDtypeStruct((count, rows, width), jnp.bfloat16)
    products = jax.ShapeDtypeStruct((states, span, width), jnp.bfloat16)
    return pl.pallas_call(
        functools.partial(own_kernel, first, sectors, wide, states, span, width, splits),
        out_shape=[block, products] if wide else [block],
        in_specs=[SMEM] + [ANY] * (2 + len(other_env)),
        out_specs=[HBM, HBM] if wide else [HBM],
        scratch_shapes=[
            pltpu.VMEM((span, span), jnp.bfloat16),
            pltpu.VMEM((2, span, width), jnp.bfloat16),
            pltpu.VMEM((slots, span, width), jnp.bfloat16),
            pltpu.VMEM((count, rows, width), jnp.bfloat16),
            pltpu.SemaphoreType.DMA((splits,)),
            pltpu.SemaphoreType.DMA((2,)),
            pltpu.SemaphoreType.DMA((count,)),
            pltpu.SemaphoreType.DMA((slots,)),
        ],
        compiler_params=PARAMS,
        cost_estimate=pl.CostEstimate(
            flops=4 * states * span * span * width, bytes_accessed=4 * count * rows * width, transcendentals=0
        ),
    )(meta, tensor, env, *other_env)


def other_terms(meta, result, products, other_tensor, states, splits):
    count, span, width = result.shape
    return pl.pallas_call(
        functools.partial(other_kernel, states, span, width, splits),
        out_shape=jax.ShapeDtypeStruct(result.shape, jnp.bfloat16),
        in_specs=[SMEM, HBM, ANY] + [ANY] * len(other_tensor),
        out_specs=HBM,
        input_output_aliases={1: 0},
        scratch_shapes=[
            pltpu.VMEM((2, max(splits - 1, 1), span, width), jnp.bfloat16),
            pltpu.VMEM((2, span, width), jnp.bfloat16),
            pltpu.VMEM((count, max(splits - 1, 1), width, width), jnp.bfloat16),
            pltpu.SemaphoreType.DMA((2, max(splits - 1, 1))),
            pltpu.SemaphoreType.DMA((2,)),
            pltpu.SemaphoreType.DMA((count, max(splits - 1, 1))),
        ],
        compiler_params=PARAMS,
    )(meta, result, products, *other_tensor)


def body(left_env, site_tensor, left_sizes, right_sizes, targets):
    splits = lax.axis_size("split")
    groups = lax.axis_size("groups")
    lanes = lax.axis_size("charge")
    tensor, env = site_tensor[0], left_env[0]
    states, span, width = tensor.shape
    sectors = right_sizes.shape[0]
    first = max(sectors * 3 // 8, 1)
    leads = sorted({max(sectors * e // 8, 1) for e in (3, 4, 5, 8)})
    shifts = [[(y, (y + h) % splits) for y in range(splits)] for h in range(1, splits)]
    depths = max(span // TILE // (splits - 1), 1) if splits > 1 else 1
    grain = span // depths
    blocks = (left_sizes[0] + grain - 1) // grain

    other_sizes = [
        lax.ppermute(right_sizes, "groups", [(g, (g + h) % groups) for g in range(groups)]) for h in range(1, groups)
    ]

    def send_env(v):
        rows = min(v * grain, width)
        senders = -(-v * grain // width)

        def branch(block):
            piece = block[:rows, : v * grain]
            got = [lax.ppermute(piece, "split", [p for p in pairs if p[0] < senders]) for pairs in shifts]
            return tuple(jnp.pad(g, ((0, width - rows), (0, span - v * grain))) for g in got)

        return branch

    other_env = lax.switch(blocks - 1, [send_env(v) for v in range(1, depths + 1)], env)
    other_env, other_sizes = lax.optimization_barrier((other_env, other_sizes))

    meta = pl.pallas_call(
        functools.partial(meta_kernel, sectors, states, width, depths, grain, leads),
        out_shape=jax.ShapeDtypeStruct((6, max(sectors, 8)), jnp.int32),
        in_specs=[SMEM] * (3 + len(other_sizes)),
        out_specs=SMEM,
    )(left_sizes, targets, right_sizes, *other_sizes)

    piece = lax.dynamic_slice(tensor, (meta[4, 0], 0, 0), (1, span, width))[0]
    slot_first = [lax.ppermute(piece, "split", pairs) for pairs in shifts]

    (small,) = own_terms(first, sectors, False, meta, tensor, env, other_env, splits)
    small, env = lax.optimization_barrier((small, env))
    small_sum = lax.psum_scatter(small, "charge", scatter_dimension=1, tiled=True)
    result, products = own_terms(first, sectors, True, meta, tensor, env, other_env, splits)
    result, tensor = lax.optimization_barrier((result, tensor))

    def send_tensor(used, v):
        def branch(block, meta):
            got = []
            for pairs in shifts:
                for i in range(1, states):
                    if i >= used:
                        got.append(
                            pl.pallas_call(
                                blank_kernel,
                                out_shape=jax.ShapeDtypeStruct((span, width), jnp.bfloat16),
                                out_specs=HBM,
                                compiler_params=PARAMS,
                            )()
                        )
                        continue
                    piece = lax.dynamic_slice(block, (meta[4, i], 0, 0), (1, v * grain, width))[0]
                    got.append(jnp.pad(lax.ppermute(piece, "split", pairs), ((0, span - v * grain), (0, 0))))
            return tuple(got)

        return branch

    branches = [send_tensor(1, 1)] + [send_tensor(u, v) for u in range(2, states + 1) for v in range(1, depths + 1)]
    more = lax.switch(meta[5, 3], branches, tensor, meta)
    other_tensor = []
    for h in range(splits - 1):
        other_tensor += [slot_first[h], *more[h * (states - 1) : (h + 1) * (states - 1)]]
    large = other_terms(meta, result, products, other_tensor, states, splits)

    def scatter(lead):
        def branch(large, small_sum, meta):
            large_sum = lax.psum_scatter(large[:lead], "charge", scatter_dimension=1, tiled=True)
            owned = [
                lax.ppermute(small_sum, "charge", [(j, j // splits) for j in range(lanes) if j % splits == p])
                for p in range(splits)
            ]
            return pl.pallas_call(
                functools.partial(finish_kernel, sectors, first, lead, width, splits),
                out_shape=jax.ShapeDtypeStruct((sectors, span // lanes, width), jnp.float32),
                in_specs=[SMEM] + [VMEM] * (1 + splits),
                out_specs=VMEM,
                compiler_params=PARAMS,
            )(meta, large_sum, *owned)

        return branch

    return lax.switch(meta[5, 2], [scatter(lead) for lead in leads], large, small_sum, meta)


def solution(mesh):
    in_specs = (
        P(("groups", "charge"), "split", None),
        P(("groups", "charge"), None, None, "split"),
        P(("groups", "charge")),
        P("groups"),
        P(("groups", "charge"), None),
    )
    out_specs = P("groups", "charge", "split")
    return jax.shard_map(body, mesh=mesh, in_specs=in_specs, out_specs=out_specs, check_vma=False)
```

```python
import functools

import jax
import jax.numpy as jnp
from jax import lax
from jax.experimental import pallas as pl
from jax.experimental.pallas import tpu as pltpu
from jax.sharding import PartitionSpec as P

TILE = 256


def meta_kernel(sectors, states, width, depths, grain, leads, left_ref, target_ref, right_ref, out_ref):

    def rank_sector(r, carry):
        size = right_ref[r]

        def count(other, total):
            bigger = (right_ref[other] > size) | ((right_ref[other] == size) & (other < r))
            return total + bigger.astype(jnp.int32)

        rank = lax.fori_loop(0, sectors, count, jnp.int32(0), unroll=True)
        out_ref[0, r] = rank
        out_ref[1, rank] = size
        out_ref[2, rank] = jnp.int32(-1)
        out_ref[3, rank] = jnp.int32(states)
        out_ref[4, r] = jnp.int32(0)
        out_ref[5, r] = jnp.int32(0)
        return carry

    lax.fori_loop(0, sectors, rank_sector, 0)
    for s in range(states):
        out_ref[2, out_ref[0, target_ref[0, s]]] = jnp.int32(s)

    def place(k, used):
        state = out_ref[2, k]
        wanted = (state >= 0) & (out_ref[1, k] > width)

        @pl.when(wanted)
        def _():
            out_ref[3, k] = used
            out_ref[4, used] = state

        return used + wanted.astype(jnp.int32)

    used = lax.fori_loop(0, sectors, place, jnp.int32(0))
    most = lax.fori_loop(
        0, sectors, lambda r, total: total + (right_ref[r] > width).astype(jnp.int32), jnp.int32(0), unroll=True
    )
    lead, choice = jnp.int32(leads[-1]), jnp.int32(0)
    for e in reversed(leads[:-1]):
        lead = jnp.where(most <= e, jnp.int32(e), lead)
    for e in leads[:-1]:
        choice = choice + (most > e).astype(jnp.int32)
    depth = (left_ref[0] + grain - 1) // grain
    out_ref[5, 0] = left_ref[0]
    out_ref[5, 1] = lead
    out_ref[5, 2] = choice
    out_ref[5, 3] = jnp.where(used <= 1, 0, 1 + (used - 2) * depths + depth - 1)


def own_kernel(first, sectors, wide, states, span, width, splits, rows, *refs):
    meta, t_hbm, own_hbm = refs[:3]
    others_e = refs[3 : 3 + splits - 1]
    at = 3 + splits - 1
    out_hbm = refs[at]
    products_hbm = refs[at + 1] if wide else None
    env, mine, product, result, env_sem, mine_sem, out_sem, product_sem = refs[at + 1 + int(wide) :]
    me = lax.axis_index("split")
    live_rows = meta[5, 0]
    tiles = (live_rows + TILE - 1) // TILE
    start = 0 if wide else first
    stop = meta[5, 1] if wide else sectors

    def source_base(h):
        return pl.multiple_of(lax.rem(me - h + splits, splits) * width, width)

    env_copies = [pltpu.make_async_copy(own_hbm, env.at[pl.ds(source_base(0), width)], env_sem.at[0])] + [
        pltpu.make_async_copy(others_e[h - 1], env.at[pl.ds(source_base(h), width)], env_sem.at[h])
        for h in range(1, splits)
    ]

    def wanted(k):
        yes = (meta[2, k] >= 0) & (meta[1, k] > me * width)
        if wide:
            return yes & ((k < first) | (meta[1, k] > width))
        return yes & (meta[1, k] <= width)

    def crossing(k):
        return wanted(k) & (meta[1, k] > width)

    def mine_copy(k):
        return pltpu.make_async_copy(t_hbm.at[meta[2, k]], mine.at[k % 2], mine_sem.at[k % 2])

    def begin(k):
        @pl.when(wanted(k))
        def _():
            mine_copy(k).start()

    core = lax.rem(lax.axis_index("charge"), 2)

    def out_copies(k):
        if not wide:
            return [pltpu.make_async_copy(result.at[k - start], out_hbm.at[k - start], out_sem.at[k - start, 0])]
        return [
            pltpu.make_async_copy(result.at[k, c], out_hbm.at[lax.rem(core + c, 2), k], out_sem.at[k, c])
            for c in range(2)
        ]

    def product_copy(k):
        return pltpu.make_async_copy(product.at[meta[3, k]], products_hbm.at[meta[3, k]], product_sem.at[meta[3, k]])

    for copy in env_copies:
        copy.start()
    begin(start)
    for copy in env_copies:
        copy.wait()

    def one(k, carry):
        size = meta[1, k]
        p = meta[3, k] if wide else 0
        i = k - start

        @pl.when(k + 1 < stop)
        def _():
            begin(k + 1)

        @pl.when(jnp.logical_not(wanted(k)))
        def _():
            result[i] = jnp.zeros(result.shape[1:], jnp.bfloat16)

        @pl.when(wanted(k))
        def _():
            mine_copy(k).wait()
            mask(mine.at[k % 2], size - me * width, live_rows, width)

            def multiply(b, carry):
                base = pl.multiple_of(b * TILE, TILE)
                value = jnp.dot(env[pl.ds(base, TILE), :], mine[k % 2], preferred_element_type=jnp.float32)
                product[p, pl.ds(base, TILE), :] = value.astype(jnp.bfloat16)
                return carry

            def clear(b, carry):
                product[p, pl.ds(pl.multiple_of(b * TILE, TILE), TILE), :] = jnp.zeros((TILE, width), jnp.bfloat16)
                return carry

            lax.fori_loop(0, tiles, multiply, 0)
            lax.fori_loop(tiles, span // TILE, clear, 0)
            if wide:
                half(split_store(result.at[i], me * width, rows), mine.at[k % 2], product.at[p], width)
            else:
                half(flat_store(result.at[i]), mine.at[k % 2], product.at[p], width)
            if wide:
                for h in range(1, splits):
                    @pl.when(jnp.logical_not((size > width) & (size > source_base(h))))
                    def _():
                        lines = width // (2 * rows)
                        at = source_base(h) // (2 * rows)
                        result[i, :, pl.ds(at, lines)] = jnp.zeros((2, lines, rows, width), jnp.bfloat16)

        for copy in out_copies(k):
            copy.start()
        if wide:
            @pl.when(crossing(k))
            def _():
                product_copy(k).start()
        return carry

    lax.fori_loop(start, stop, one, 0)

    def finish(k, carry):
        for copy in out_copies(k):
            copy.wait()
        if wide:
            @pl.when(crossing(k))
            def _():
                product_copy(k).wait()
        return carry

    lax.fori_loop(start, stop, finish, 0)


def mask(ref, cols, live_rows, width):
    def step(b, carry):
        base = pl.multiple_of(b * TILE, TILE)
        rows_here = lax.broadcasted_iota(jnp.int32, (TILE, width), 0) + base
        cols_here = lax.broadcasted_iota(jnp.int32, (TILE, width), 1)
        keep = (rows_here < live_rows) & (cols_here < cols)
        ref[pl.ds(base, TILE), :] = jnp.where(keep, ref[pl.ds(base, TILE), :], jnp.zeros((), jnp.bfloat16))
        return carry

    lax.fori_loop(0, ref.shape[0] // TILE, step, 0)


def flat_store(ref):
    def store(base, value):
        ref[pl.ds(pl.multiple_of(base, TILE), TILE), :] = value

    return store


def split_store(ref, row_base, rows):
    def store(base, value):
        block = (row_base + base) // (2 * rows)
        for q in range(TILE // rows):
            ref[q % 2, block + q // 2] = value[q * rows : (q + 1) * rows]

    return store


def half(store, factor, product, width):
    def step(j, carry):
        base = pl.multiple_of(j * TILE, TILE)
        value = lax.dot_general(
            factor[:, pl.ds(base, TILE)], product[...], (((0,), (0,)), ((), ())), preferred_element_type=jnp.float32
        )
        store(base, value.astype(jnp.bfloat16))
        return carry

    lax.fori_loop(0, width // TILE, step, 0)


def other_kernel(states, span, width, splits, rows, *refs):
    meta, products_hbm = refs[0], refs[2]
    others_t = refs[3 : 3 + (splits - 1) * states]
    out_hbm, theirs, product, result, theirs_sem, product_sem, out_sem = refs[3 + len(others_t) :]
    me = lax.axis_index("split")
    live_rows = meta[5, 0]
    stop = meta[5, 1]

    def source_base(h):
        return pl.multiple_of(lax.rem(me - h + splits, splits) * width, width)

    def crossing(k):
        return (meta[2, k] >= 0) & (meta[1, k] > me * width) & (meta[1, k] > width)

    def wanted(k, h):
        return crossing(k) & (meta[1, k] > source_base(h))

    def product_copy(k):
        return pltpu.make_async_copy(products_hbm.at[meta[3, k]], product.at[k % 2], product_sem.at[k % 2])

    def theirs_copy(k, h, slot):
        return pltpu.make_async_copy(others_t[(h - 1) * states + slot], theirs.at[k % 2, h - 1], theirs_sem.at[k % 2, h - 1])

    core = lax.rem(lax.axis_index("charge"), 2)
    lines = width // (2 * rows)

    def out_copies(k, h):
        at = source_base(h) // (2 * rows)
        return [
            pltpu.make_async_copy(
                result.at[k, h - 1, c], out_hbm.at[lax.rem(core + c, 2), k, pl.ds(at, lines)], out_sem.at[k, h - 1, c]
            )
            for c in range(2)
        ]

    def begin(k):
        @pl.when(crossing(k))
        def _():
            product_copy(k).start()
            for slot in range(states):
                @pl.when(meta[3, k] == slot)
                def _():
                    for h in range(1, splits):
                        theirs_copy(k, h, slot).start()

    begin(0)

    def one(k, carry):
        @pl.when(k + 1 < stop)
        def _():
            begin(k + 1)

        @pl.when(crossing(k))
        def _():
            product_copy(k).wait()
            for h in range(1, splits):
                theirs_copy(k, h, 0).wait()
            for h in range(1, splits):
                @pl.when(wanted(k, h))
                def _():
                    mask(theirs.at[k % 2, h - 1], meta[1, k] - source_base(h), live_rows, width)
                    store = split_store(result.at[k, h - 1], 0, rows)
                    half(store, theirs.at[k % 2, h - 1], product.at[k % 2], width)
                    for copy in out_copies(k, h):
                        copy.start()

        return carry

    lax.fori_loop(0, stop, one, 0)

    def finish(k, carry):
        for h in range(1, splits):
            @pl.when(wanted(k, h))
            def _():
                for copy in out_copies(k, h):
                    copy.wait()
        return carry

    lax.fori_loop(0, stop, finish, 0)


def finish_kernel(sectors, first, lead, width, pieces, meta, large_ref, *refs):
    small, out_ref = refs[:pieces], refs[pieces]
    rows = out_ref.shape[1] // pieces
    for r in range(sectors):
        rank = meta[0, r]
        in_second = (rank < first) | (meta[1, rank] > width)

        @pl.when(in_second)
        def _():
            out_ref[r] = large_ref[jnp.minimum(rank, lead - 1)]

        @pl.when(jnp.logical_not(in_second))
        def _():
            for p in range(pieces):
                out_ref[r, p * rows : (p + 1) * rows, :] = small[p][jnp.maximum(rank - first, 0)].astype(jnp.float32)


def blank_kernel(out_ref):
    pass


ANY = pl.BlockSpec(memory_space=pl.ANY)
HBM = pl.BlockSpec(memory_space=pltpu.HBM)
SMEM = pl.BlockSpec(memory_space=pltpu.SMEM)
VMEM = pl.BlockSpec(memory_space=pltpu.VMEM)
PARAMS = pltpu.CompilerParams(vmem_limit_bytes=62 * 1024 * 1024)


def own_terms(first, sectors, wide, meta, tensor, env, other_env, splits, lanes):
    states, span, width = tensor.shape
    share = span // lanes
    shape = (2, sectors, lanes // 2, share, width) if wide else (sectors - first, width, width)
    held = (sectors, 2, lanes // 2, share, width) if wide else shape
    slots = states + 1 if wide else 1
    block = jax.ShapeDtypeStruct(shape, jnp.bfloat16)
    products = jax.ShapeDtypeStruct((states, span, width), jnp.bfloat16)
    return pl.pallas_call(
        functools.partial(own_kernel, first, sectors, wide, states, span, width, splits, share),
        out_shape=[block, products] if wide else [block],
        in_specs=[SMEM] + [ANY] * (2 + len(other_env)),
        out_specs=[HBM, HBM] if wide else [HBM],
        scratch_shapes=[
            pltpu.VMEM((span, span), jnp.bfloat16),
            pltpu.VMEM((2, span, width), jnp.bfloat16),
            pltpu.VMEM((slots, span, width), jnp.bfloat16),
            pltpu.VMEM(held, jnp.bfloat16),
            pltpu.SemaphoreType.DMA((splits,)),
            pltpu.SemaphoreType.DMA((2,)),
            pltpu.SemaphoreType.DMA((held[0], 2)),
            pltpu.SemaphoreType.DMA((slots,)),
        ],
        compiler_params=PARAMS,
        cost_estimate=pl.CostEstimate(
            flops=(1 if wide else 8) * states * span * span * width, bytes_accessed=4 * span * width, transcendentals=0
        ),
    )(meta, tensor, env, *other_env)


def other_terms(meta, result, products, other_tensor, states, splits):
    sectors, chips, share, width = result.shape[1:]
    span = 2 * chips * share
    others = max(splits - 1, 1)
    return pl.pallas_call(
        functools.partial(other_kernel, states, span, width, splits, share),
        out_shape=jax.ShapeDtypeStruct(result.shape, jnp.bfloat16),
        in_specs=[SMEM, HBM, ANY] + [ANY] * len(other_tensor),
        out_specs=HBM,
        input_output_aliases={1: 0},
        scratch_shapes=[
            pltpu.VMEM((2, others, span, width), jnp.bfloat16),
            pltpu.VMEM((2, span, width), jnp.bfloat16),
            pltpu.VMEM((sectors, others, 2, width // (2 * share), share, width), jnp.bfloat16),
            pltpu.SemaphoreType.DMA((2, others)),
            pltpu.SemaphoreType.DMA((2,)),
            pltpu.SemaphoreType.DMA((sectors, others, 2)),
        ],
        compiler_params=PARAMS,
    )(meta, result, products, *other_tensor)


def line_scatter(terms, theirs, lanes):
    chips = lanes // 2
    chip = lax.axis_index("charge") // 2

    def pick(d):
        d = jnp.clip(d, 0, chips - 1)
        lead, share, width = theirs.shape[0], theirs.shape[2], theirs.shape[3]
        mine = lax.dynamic_slice(terms, (0, 0, d, 0, 0), (1, lead, 1, share, width))[0, :, 0]
        return mine.astype(jnp.float32) + lax.dynamic_index_in_dim(theirs, d, 1, keepdims=False).astype(jnp.float32)

    carried = [None, None]
    for t in range(1, chips):
        values = []
        for way in range(2):
            value = pick(chips - t + chip if way == 0 else t - chips + chip)
            if carried[way] is not None:
                value = value + carried[way].astype(jnp.float32)
            values.append(value.astype(jnp.bfloat16))
        values = lax.optimization_barrier(values)
        for way in range(2):
            places = range(t) if way == 0 else range(chips - t, chips)
            hop = 1 if way == 0 else -1
            pairs = [(2 * z + c, 2 * (z + hop) + c) for z in places for c in range(2)]
            carried[way] = lax.ppermute(values[way], "charge", pairs)
    total = pick(chip)
    for part in carried:
        if part is not None:
            total = total + part.astype(jnp.float32)
    return total


def body(left_env, site_tensor, left_sizes, right_sizes, targets):
    splits = lax.axis_size("split")
    lanes = lax.axis_size("charge")
    tensor, env = site_tensor[0], left_env[0]
    states, span, width = tensor.shape
    sectors = right_sizes.shape[0]
    first = max(sectors * 3 // 8, 1)
    leads = sorted({max(sectors * e // 8, 1) for e in (3, 4, 5, 8)})
    shifts = [[(y, (y + h) % splits) for y in range(splits)] for h in range(1, splits)]
    depths = max(span // TILE // (splits - 1), 1) if splits > 1 else 1
    grain = span // depths
    blocks = (left_sizes[0] + grain - 1) // grain

    def send_env(v):
        rows = min(v * grain, width)
        senders = -(-v * grain // width)

        def branch(block):
            piece = block[:rows, : v * grain]
            got = [lax.ppermute(piece, "split", [p for p in pairs if p[0] < senders]) for pairs in shifts]
            return tuple(jnp.pad(g, ((0, width - rows), (0, span - v * grain))) for g in got)

        return branch

    other_env = lax.switch(blocks - 1, [send_env(v) for v in range(1, depths + 1)], env)

    meta = pl.pallas_call(
        functools.partial(meta_kernel, sectors, states, width, depths, grain, leads),
        out_shape=jax.ShapeDtypeStruct((6, max(sectors, 8)), jnp.int32),
        in_specs=[SMEM] * 3,
        out_specs=SMEM,
    )(left_sizes, targets, right_sizes)

    piece = lax.dynamic_slice(tensor, (meta[4, 0], 0, 0), (1, span, width))[0]
    slot_first = [lax.ppermute(piece, "split", pairs) for pairs in shifts]

    (small,) = own_terms(first, sectors, False, meta, tensor, env, other_env, splits, lanes)
    small, env = lax.optimization_barrier((small, env))
    small_sum = lax.psum_scatter(small, "charge", scatter_dimension=1, tiled=True)
    result, products = own_terms(first, sectors, True, meta, tensor, env, other_env, splits, lanes)
    result, tensor = lax.optimization_barrier((result, tensor))

    def send_tensor(used, v):
        def branch(block, meta):
            got = []
            for pairs in shifts:
                for i in range(1, states):
                    if i >= used:
                        got.append(
                            pl.pallas_call(
                                blank_kernel,
                                out_shape=jax.ShapeDtypeStruct((span, width), jnp.bfloat16),
                                out_specs=HBM,
                                compiler_params=PARAMS,
                            )()
                        )
                        continue
                    piece = lax.dynamic_slice(block, (meta[4, i], 0, 0), (1, v * grain, width))[0]
                    got.append(jnp.pad(lax.ppermute(piece, "split", pairs), ((0, span - v * grain), (0, 0))))
            return tuple(got)

        return branch

    branches = [send_tensor(1, 1)] + [send_tensor(u, v) for u in range(2, states + 1) for v in range(1, depths + 1)]
    more = lax.switch(meta[5, 3], branches, tensor, meta)
    other_tensor = []
    for h in range(splits - 1):
        other_tensor += [slot_first[h], *more[h * (states - 1) : (h + 1) * (states - 1)]]
    large = other_terms(meta, result, products, other_tensor, states, splits)

    def scatter(lead):
        def branch(large, small_sum, meta):
            swapped = lax.ppermute(large[1, :lead], "charge", [(j, j ^ 1) for j in range(lanes)])
            large_sum = line_scatter(large, swapped, lanes)
            owned = [
                lax.ppermute(small_sum, "charge", [(j, j // splits) for j in range(lanes) if j % splits == p])
                for p in range(splits)
            ]
            return pl.pallas_call(
                functools.partial(finish_kernel, sectors, first, lead, width, splits),
                out_shape=jax.ShapeDtypeStruct((sectors, span // lanes, width), jnp.float32),
                in_specs=[SMEM] + [VMEM] * (1 + splits),
                out_specs=VMEM,
                compiler_params=PARAMS,
            )(meta, large_sum, *owned)

        return branch

    return lax.switch(meta[5, 2], [scatter(lead) for lead in leads], large, small_sum, meta)


def solution(mesh):
    in_specs = (
        P(("groups", "charge"), "split", None),
        P(("groups", "charge"), None, None, "split"),
        P(("groups", "charge")),
        P("groups"),
        P(("groups", "charge"), None),
    )
    out_specs = P("groups", "charge", "split")
    return jax.shard_map(body, mesh=mesh, in_specs=in_specs, out_specs=out_specs, check_vma=False)
```

```python
import functools

import jax
import jax.numpy as jnp
from jax import lax
from jax.experimental import pallas as pl
from jax.experimental.pallas import tpu as pltpu
from jax.sharding import PartitionSpec as P

TILE = 256


def meta_kernel(sectors, states, width, depths, grain, leads, left_ref, target_ref, right_ref, out_ref):

    def rank_sector(r, carry):
        size = right_ref[r]

        def count(other, total):
            bigger = (right_ref[other] > size) | ((right_ref[other] == size) & (other < r))
            return total + bigger.astype(jnp.int32)

        rank = lax.fori_loop(0, sectors, count, jnp.int32(0), unroll=True)
        out_ref[0, r] = rank
        out_ref[1, rank] = size
        out_ref[2, rank] = jnp.int32(-1)
        out_ref[3, rank] = jnp.int32(states)
        out_ref[4, r] = jnp.int32(0)
        out_ref[5, r] = jnp.int32(0)
        return carry

    lax.fori_loop(0, sectors, rank_sector, 0)
    for s in range(states):
        out_ref[2, out_ref[0, target_ref[0, s]]] = jnp.int32(s)

    def place(k, used):
        state = out_ref[2, k]
        wanted = (state >= 0) & (out_ref[1, k] > width)

        @pl.when(wanted)
        def _():
            out_ref[3, k] = used
            out_ref[4, used] = state

        return used + wanted.astype(jnp.int32)

    used = lax.fori_loop(0, sectors, place, jnp.int32(0))
    most = lax.fori_loop(
        0, sectors, lambda r, total: total + (right_ref[r] > width).astype(jnp.int32), jnp.int32(0), unroll=True
    )
    lead, choice = jnp.int32(leads[-1]), jnp.int32(0)
    for e in reversed(leads[:-1]):
        lead = jnp.where(most <= e, jnp.int32(e), lead)
    for e in leads[:-1]:
        choice = choice + (most > e).astype(jnp.int32)
    depth = (left_ref[0] + grain - 1) // grain
    out_ref[5, 0] = left_ref[0]
    out_ref[5, 1] = lead
    out_ref[5, 2] = choice
    out_ref[5, 3] = jnp.where(used <= 1, 0, 1 + (used - 2) * depths + depth - 1)


def own_kernel(first, sectors, states, span, width, splits, rows, *refs):
    meta, t_hbm, own_hbm = refs[:3]
    others_e = refs[3 : 3 + splits - 1]
    small_hbm, wide_hbm, products_hbm = refs[2 + splits : 5 + splits]
    env, mine, product, small, wide, env_sem, mine_sem, small_sem, wide_sem, product_sem = refs[5 + splits :]
    me = lax.axis_index("split")
    core = lax.rem(lax.axis_index("charge"), 2)
    live_rows = meta[5, 0]
    lead = meta[5, 1]
    tiles = (live_rows + TILE - 1) // TILE

    def source_base(h):
        return pl.multiple_of(lax.rem(me - h + splits, splits) * width, width)

    env_copies = [pltpu.make_async_copy(own_hbm, env.at[pl.ds(source_base(0), width)], env_sem.at[0])] + [
        pltpu.make_async_copy(others_e[h - 1], env.at[pl.ds(source_base(h), width)], env_sem.at[h])
        for h in range(1, splits)
    ]

    def some(k):
        return (meta[2, k] >= 0) & (meta[1, k] > me * width)

    def small_wanted(k):
        return some(k) & (meta[1, k] <= width)

    def wide_wanted(k):
        return some(k) & ((k < first) | (meta[1, k] > width))

    def crossing(k):
        return some(k) & (meta[1, k] > width)

    def mine_copy(k):
        return pltpu.make_async_copy(t_hbm.at[meta[2, k]], mine.at[k % 2], mine_sem.at[k % 2])

    def begin(k, wanted):
        @pl.when(wanted(k))
        def _():
            mine_copy(k).start()

    def small_copy(k):
        return pltpu.make_async_copy(small.at[k - first], small_hbm.at[k - first], small_sem.at[k - first])

    def wide_copies(k):
        return [
            pltpu.make_async_copy(wide.at[k, c], wide_hbm.at[lax.rem(core + c, 2), k], wide_sem.at[k, c])
            for c in range(2)
        ]

    def product_copy(k):
        return pltpu.make_async_copy(product.at[meta[3, k]], products_hbm.at[meta[3, k]], product_sem.at[meta[3, k]])

    def multiply(k, p):
        mine_copy(k).wait()
        mask(mine.at[k % 2], meta[1, k] - me * width, live_rows, width)

        def step(b, carry):
            base = pl.multiple_of(b * TILE, TILE)
            value = jnp.dot(env[pl.ds(base, TILE), :], mine[k % 2], preferred_element_type=jnp.float32)
            product[p, pl.ds(base, TILE), :] = value.astype(jnp.bfloat16)
            return carry

        def clear(b, carry):
            product[p, pl.ds(pl.multiple_of(b * TILE, TILE), TILE), :] = jnp.zeros((TILE, width), jnp.bfloat16)
            return carry

        lax.fori_loop(0, tiles, step, 0)
        lax.fori_loop(tiles, span // TILE, clear, 0)

    for copy in env_copies:
        copy.start()
    begin(first, small_wanted)
    for copy in env_copies:
        copy.wait()

    def one_small(k, carry):
        @pl.when(k + 1 < sectors)
        def _():
            begin(k + 1, small_wanted)

        @pl.when(jnp.logical_not(small_wanted(k)))
        def _():
            small[k - first] = jnp.zeros((width, width), jnp.bfloat16)

        @pl.when(small_wanted(k))
        def _():
            multiply(k, states)
            half(flat_store(small.at[k - first]), mine.at[k % 2], product.at[states], width)

        small_copy(k).start()
        return carry

    lax.fori_loop(first, sectors, one_small, 0)
    begin(0, wide_wanted)

    def one_wide(k, carry):
        size = meta[1, k]
        p = meta[3, k]

        @pl.when(k + 1 < lead)
        def _():
            begin(k + 1, wide_wanted)

        @pl.when(jnp.logical_not(wide_wanted(k)))
        def _():
            wide[k] = jnp.zeros(wide.shape[1:], jnp.bfloat16)

        @pl.when(wide_wanted(k))
        def _():
            multiply(k, p)
            half(split_store(wide.at[k], me * width, rows), mine.at[k % 2], product.at[p], width)
            for h in range(1, splits):
                @pl.when(jnp.logical_not((size > width) & (size > source_base(h))))
                def _():
                    lines = width // (2 * rows)
                    at = source_base(h) // (2 * rows)
                    wide[k, :, pl.ds(at, lines)] = jnp.zeros((2, lines, rows, width), jnp.bfloat16)

        for copy in wide_copies(k):
            copy.start()

        @pl.when(crossing(k))
        def _():
            product_copy(k).start()

        return carry

    lax.fori_loop(0, lead, one_wide, 0)

    def end_small(k, carry):
        small_copy(k).wait()
        return carry

    def end_wide(k, carry):
        for copy in wide_copies(k):
            copy.wait()

        @pl.when(crossing(k))
        def _():
            product_copy(k).wait()

        return carry

    lax.fori_loop(first, sectors, end_small, 0)
    lax.fori_loop(0, lead, end_wide, 0)


def mask(ref, cols, live_rows, width):
    def step(b, carry):
        base = pl.multiple_of(b * TILE, TILE)
        rows_here = lax.broadcasted_iota(jnp.int32, (TILE, width), 0) + base
        cols_here = lax.broadcasted_iota(jnp.int32, (TILE, width), 1)
        keep = (rows_here < live_rows) & (cols_here < cols)
        ref[pl.ds(base, TILE), :] = jnp.where(keep, ref[pl.ds(base, TILE), :], jnp.zeros((), jnp.bfloat16))
        return carry

    lax.fori_loop(0, ref.shape[0] // TILE, step, 0)


def flat_store(ref):
    def store(base, value):
        ref[pl.ds(pl.multiple_of(base, TILE), TILE), :] = value

    return store


def split_store(ref, row_base, rows):
    def store(base, value):
        block = (row_base + base) // (2 * rows)
        for q in range(TILE // rows):
            ref[q % 2, block + q // 2] = value[q * rows : (q + 1) * rows]

    return store


def half(store, factor, product, width):
    def step(j, carry):
        base = pl.multiple_of(j * TILE, TILE)
        value = lax.dot_general(
            factor[:, pl.ds(base, TILE)], product[...], (((0,), (0,)), ((), ())), preferred_element_type=jnp.float32
        )
        store(base, value.astype(jnp.bfloat16))
        return carry

    lax.fori_loop(0, width // TILE, step, 0)


def other_kernel(states, span, width, splits, rows, *refs):
    meta, products_hbm = refs[0], refs[2]
    others_t = refs[3 : 3 + (splits - 1) * states]
    out_hbm, theirs, product, result, theirs_sem, product_sem, out_sem = refs[3 + len(others_t) :]
    me = lax.axis_index("split")
    live_rows = meta[5, 0]
    stop = meta[5, 1]

    def source_base(h):
        return pl.multiple_of(lax.rem(me - h + splits, splits) * width, width)

    def crossing(k):
        return (meta[2, k] >= 0) & (meta[1, k] > me * width) & (meta[1, k] > width)

    def wanted(k, h):
        return crossing(k) & (meta[1, k] > source_base(h))

    def product_copy(k):
        return pltpu.make_async_copy(products_hbm.at[meta[3, k]], product.at[k % 2], product_sem.at[k % 2])

    def theirs_copy(k, h, slot):
        return pltpu.make_async_copy(others_t[(h - 1) * states + slot], theirs.at[k % 2, h - 1], theirs_sem.at[k % 2, h - 1])

    core = lax.rem(lax.axis_index("charge"), 2)
    lines = width // (2 * rows)

    def out_copies(k, h):
        at = source_base(h) // (2 * rows)
        return [
            pltpu.make_async_copy(
                result.at[k, h - 1, c], out_hbm.at[lax.rem(core + c, 2), k, pl.ds(at, lines)], out_sem.at[k, h - 1, c]
            )
            for c in range(2)
        ]

    def begin(k):
        @pl.when(crossing(k))
        def _():
            product_copy(k).start()
            for slot in range(states):
                @pl.when(meta[3, k] == slot)
                def _():
                    for h in range(1, splits):
                        theirs_copy(k, h, slot).start()

    begin(0)

    def one(k, carry):
        @pl.when(k + 1 < stop)
        def _():
            begin(k + 1)

        @pl.when(crossing(k))
        def _():
            product_copy(k).wait()
            for h in range(1, splits):
                theirs_copy(k, h, 0).wait()
            for h in range(1, splits):
                @pl.when(wanted(k, h))
                def _():
                    mask(theirs.at[k % 2, h - 1], meta[1, k] - source_base(h), live_rows, width)
                    store = split_store(result.at[k, h - 1], 0, rows)
                    half(store, theirs.at[k % 2, h - 1], product.at[k % 2], width)
                    for copy in out_copies(k, h):
                        copy.start()

        return carry

    lax.fori_loop(0, stop, one, 0)

    def finish(k, carry):
        for h in range(1, splits):
            @pl.when(wanted(k, h))
            def _():
                for copy in out_copies(k, h):
                    copy.wait()
        return carry

    lax.fori_loop(0, stop, finish, 0)


def place_wide_kernel(sectors, first, lead, width, meta, large_ref, out_ref):
    for r in range(sectors):
        rank = meta[0, r]

        @pl.when((rank < first) | (meta[1, rank] > width))
        def _():
            out_ref[r] = large_ref[jnp.minimum(rank, lead - 1)]


def place_small_kernel(sectors, first, width, pieces, meta, held_ref, *refs):
    small, (out_hbm, cast, sem) = refs[:pieces], refs[pieces:]
    rows = cast.shape[1] // pieces

    def copy(r):
        return pltpu.make_async_copy(cast.at[r], out_hbm.at[r], sem.at[r])

    def is_small(r):
        rank = meta[0, r]
        return (rank >= first) & (meta[1, rank] <= width)

    for r in range(sectors):
        @pl.when(is_small(r))
        def _():
            rank = jnp.maximum(meta[0, r] - first, 0)
            for p in range(pieces):
                cast[r, p * rows : (p + 1) * rows, :] = small[p][rank].astype(jnp.float32)
            copy(r).start()

    for r in range(sectors):
        @pl.when(is_small(r))
        def _():
            copy(r).wait()


def blank_kernel(out_ref):
    pass


ANY = pl.BlockSpec(memory_space=pl.ANY)
HBM = pl.BlockSpec(memory_space=pltpu.HBM)
SMEM = pl.BlockSpec(memory_space=pltpu.SMEM)
VMEM = pl.BlockSpec(memory_space=pltpu.VMEM)
PARAMS = pltpu.CompilerParams(vmem_limit_bytes=62 * 1024 * 1024)


def own_terms(first, sectors, meta, tensor, env, other_env, splits, lanes):
    states, span, width = tensor.shape
    share = span // lanes
    small = jax.ShapeDtypeStruct((sectors - first, width, width), jnp.bfloat16)
    wide = jax.ShapeDtypeStruct((2, sectors, lanes // 2, share, width), jnp.bfloat16)
    products = jax.ShapeDtypeStruct((states, span, width), jnp.bfloat16)
    return pl.pallas_call(
        functools.partial(own_kernel, first, sectors, states, span, width, splits, share),
        out_shape=[small, wide, products],
        in_specs=[SMEM] + [ANY] * (2 + len(other_env)),
        out_specs=[HBM] * 3,
        scratch_shapes=[
            pltpu.VMEM((span, span), jnp.bfloat16),
            pltpu.VMEM((2, span, width), jnp.bfloat16),
            pltpu.VMEM((states + 1, span, width), jnp.bfloat16),
            pltpu.VMEM(small.shape, jnp.bfloat16),
            pltpu.VMEM((sectors, 2, lanes // 2, share, width), jnp.bfloat16),
            pltpu.SemaphoreType.DMA((splits,)),
            pltpu.SemaphoreType.DMA((2,)),
            pltpu.SemaphoreType.DMA((sectors - first,)),
            pltpu.SemaphoreType.DMA((sectors, 2)),
            pltpu.SemaphoreType.DMA((states + 1,)),
        ],
        compiler_params=PARAMS,
        cost_estimate=pl.CostEstimate(
            flops=4 * states * span * span * width, bytes_accessed=8 * span * width, transcendentals=0
        ),
    )(meta, tensor, env, *other_env)


def other_terms(meta, result, products, other_tensor, states, splits):
    sectors, chips, share, width = result.shape[1:]
    span = 2 * chips * share
    others = max(splits - 1, 1)
    return pl.pallas_call(
        functools.partial(other_kernel, states, span, width, splits, share),
        out_shape=jax.ShapeDtypeStruct(result.shape, jnp.bfloat16),
        in_specs=[SMEM, HBM, ANY] + [ANY] * len(other_tensor),
        out_specs=HBM,
        input_output_aliases={1: 0},
        scratch_shapes=[
            pltpu.VMEM((2, others, span, width), jnp.bfloat16),
            pltpu.VMEM((2, span, width), jnp.bfloat16),
            pltpu.VMEM((sectors, others, 2, width // (2 * share), share, width), jnp.bfloat16),
            pltpu.SemaphoreType.DMA((2, others)),
            pltpu.SemaphoreType.DMA((2,)),
            pltpu.SemaphoreType.DMA((sectors, others, 2)),
        ],
        compiler_params=PARAMS,
    )(meta, result, products, *other_tensor)


def line_scatter(terms, theirs, lanes):
    chips = lanes // 2
    chip = lax.axis_index("charge") // 2

    def pick(d):
        d = jnp.clip(d, 0, chips - 1)
        lead, share, width = theirs.shape[0], theirs.shape[2], theirs.shape[3]
        mine = lax.dynamic_slice(terms, (0, 0, d, 0, 0), (1, lead, 1, share, width))[0, :, 0]
        return mine.astype(jnp.float32) + lax.dynamic_index_in_dim(theirs, d, 1, keepdims=False).astype(jnp.float32)

    carried = [None, None]
    for t in range(1, chips):
        values = []
        for way in range(2):
            value = pick(chips - t + chip if way == 0 else t - chips + chip)
            if carried[way] is not None:
                value = value + carried[way].astype(jnp.float32)
            values.append(value.astype(jnp.bfloat16))
        values = lax.optimization_barrier(values)
        for way in range(2):
            places = range(t) if way == 0 else range(chips - t, chips)
            hop = 1 if way == 0 else -1
            pairs = [(2 * z + c, 2 * (z + hop) + c) for z in places for c in range(2)]
            carried[way] = lax.ppermute(values[way], "charge", pairs)
    total = pick(chip)
    for part in carried:
        if part is not None:
            total = total + part.astype(jnp.float32)
    return total


def body(left_env, site_tensor, left_sizes, right_sizes, targets):
    splits = lax.axis_size("split")
    lanes = lax.axis_size("charge")
    tensor, env = site_tensor[0], left_env[0]
    states, span, width = tensor.shape
    sectors = right_sizes.shape[0]
    first = max(sectors * 3 // 8, 1)
    leads = sorted({max(sectors * e // 8, 1) for e in (3, 4, 5, 8)})
    shifts = [[(y, (y + h) % splits) for y in range(splits)] for h in range(1, splits)]
    depths = max(span // TILE // (splits - 1), 1) if splits > 1 else 1
    grain = span // depths
    blocks = (left_sizes[0] + grain - 1) // grain

    def send_env(v):
        rows = min(v * grain, width)
        senders = -(-v * grain // width)

        def branch(block):
            piece = block[:rows, : v * grain]
            got = [lax.ppermute(piece, "split", [p for p in pairs if p[0] < senders]) for pairs in shifts]
            return tuple(jnp.pad(g, ((0, width - rows), (0, span - v * grain))) for g in got)

        return branch

    other_env = lax.switch(blocks - 1, [send_env(v) for v in range(1, depths + 1)], env)

    meta = pl.pallas_call(
        functools.partial(meta_kernel, sectors, states, width, depths, grain, leads),
        out_shape=jax.ShapeDtypeStruct((6, max(sectors, 8)), jnp.int32),
        in_specs=[SMEM] * 3,
        out_specs=SMEM,
    )(left_sizes, targets, right_sizes)

    piece = lax.dynamic_slice(tensor, (meta[4, 0], 0, 0), (1, span, width))[0]
    piece, other_env = lax.optimization_barrier((piece, other_env))
    slot_first = [lax.ppermute(piece, "split", pairs) for pairs in shifts]

    small, result, products = own_terms(first, sectors, meta, tensor, env, other_env, splits, lanes)
    small, result, tensor, slot_first = lax.optimization_barrier((small, result, tensor, slot_first))
    small_sum = lax.psum_scatter(small, "charge", scatter_dimension=1, tiled=True)

    def send_tensor(used, v):
        def branch(block, meta):
            got = []
            for pairs in shifts:
                for i in range(1, states):
                    if i >= used:
                        got.append(
                            pl.pallas_call(
                                blank_kernel,
                                out_shape=jax.ShapeDtypeStruct((span, width), jnp.bfloat16),
                                out_specs=HBM,
                                compiler_params=PARAMS,
                            )()
                        )
                        continue
                    piece = lax.dynamic_slice(block, (meta[4, i], 0, 0), (1, v * grain, width))[0]
                    got.append(jnp.pad(lax.ppermute(piece, "split", pairs), ((0, span - v * grain), (0, 0))))
            return tuple(got)

        return branch

    branches = [send_tensor(1, 1)] + [send_tensor(u, v) for u in range(2, states + 1) for v in range(1, depths + 1)]
    more = lax.switch(meta[5, 3], branches, tensor, meta)
    other_tensor = []
    for h in range(splits - 1):
        other_tensor += [slot_first[h], *more[h * (states - 1) : (h + 1) * (states - 1)]]
    large = other_terms(meta, result, products, other_tensor, states, splits)

    def scatter(lead):
        def branch(large, meta):
            swapped = lax.ppermute(large[1, :lead], "charge", [(j, j ^ 1) for j in range(lanes)])
            return pl.pallas_call(
                functools.partial(place_wide_kernel, sectors, first, lead, width),
                out_shape=jax.ShapeDtypeStruct((sectors, span // lanes, width), jnp.float32),
                in_specs=[SMEM, VMEM],
                out_specs=VMEM,
                compiler_params=PARAMS,
            )(meta, line_scatter(large, swapped, lanes))

        return branch

    held = lax.switch(meta[5, 2], [scatter(lead) for lead in leads], large, meta)
    held, small_sum = lax.optimization_barrier((held, small_sum))
    owned = [
        lax.ppermute(small_sum, "charge", [(j, j // splits) for j in range(lanes) if j % splits == p])
        for p in range(splits)
    ]
    return pl.pallas_call(
        functools.partial(place_small_kernel, sectors, first, width, splits),
        out_shape=jax.ShapeDtypeStruct(held.shape, jnp.float32),
        in_specs=[SMEM, HBM] + [VMEM] * splits,
        out_specs=HBM,
        input_output_aliases={1: 0},
        scratch_shapes=[pltpu.VMEM(held.shape, jnp.float32), pltpu.SemaphoreType.DMA((sectors,))],
        compiler_params=PARAMS,
    )(meta, held, *owned)


def solution(mesh):
    in_specs = (
        P(("groups", "charge"), "split", None),
        P(("groups", "charge"), None, None, "split"),
        P(("groups", "charge")),
        P("groups"),
        P(("groups", "charge"), None),
    )
    out_specs = P("groups", "charge", "split")
    return jax.shard_map(body, mesh=mesh, in_specs=in_specs, out_specs=out_specs, check_vma=False)
```

```python
import functools

import jax
import jax.numpy as jnp
from jax import lax
from jax.experimental import pallas as pl
from jax.experimental.pallas import tpu as pltpu
from jax.sharding import PartitionSpec as P

TILE = 256


def meta_kernel(sectors, states, width, depths, grain, leads, left_ref, target_ref, right_ref, *refs):
    others, out_ref = refs[:-1], refs[-1]

    def rank_sector(r, carry):
        size = right_ref[r]

        def count(other, total):
            bigger = (right_ref[other] > size) | ((right_ref[other] == size) & (other < r))
            return total + bigger.astype(jnp.int32)

        rank = lax.fori_loop(0, sectors, count, jnp.int32(0), unroll=True)
        out_ref[0, r] = rank
        out_ref[1, rank] = size
        out_ref[2, rank] = jnp.int32(-1)
        out_ref[3, rank] = jnp.int32(states)
        out_ref[4, r] = jnp.int32(0)
        out_ref[5, r] = jnp.int32(0)
        return carry

    lax.fori_loop(0, sectors, rank_sector, 0)
    for s in range(states):
        out_ref[2, out_ref[0, target_ref[0, s]]] = jnp.int32(s)

    def place(k, used):
        state = out_ref[2, k]
        wanted = (state >= 0) & (out_ref[1, k] > width)

        @pl.when(wanted)
        def _():
            out_ref[3, k] = used
            out_ref[4, used] = state

        return used + wanted.astype(jnp.int32)

    used = lax.fori_loop(0, sectors, place, jnp.int32(0))
    most = jnp.int32(0)
    for ref in (right_ref,) + others:
        def wide(r, total, ref=ref):
            return total + (ref[r] > width).astype(jnp.int32)

        most = jnp.maximum(most, lax.fori_loop(0, sectors, wide, jnp.int32(0), unroll=True))
    lead, choice = jnp.int32(leads[-1]), jnp.int32(0)
    for e in reversed(leads[:-1]):
        lead = jnp.where(most <= e, jnp.int32(e), lead)
    for e in leads[:-1]:
        choice = choice + (most > e).astype(jnp.int32)
    depth = (left_ref[0] + grain - 1) // grain
    out_ref[5, 0] = left_ref[0]
    out_ref[5, 1] = lead
    out_ref[5, 2] = choice
    out_ref[5, 3] = jnp.where(used <= 1, 0, 1 + (used - 2) * depths + depth - 1)


def own_kernel(first, sectors, states, span, width, splits, *refs):
    meta, t_hbm, own_hbm = refs[:3]
    others_e = refs[3 : 3 + splits - 1]
    small_hbm, low_hbm, high_hbm, products_hbm = refs[2 + splits : 6 + splits]
    env, mine, product, small, wide, env_sem, mine_sem, small_sem, wide_sem, product_sem = refs[6 + splits :]
    me = lax.axis_index("split")
    live_rows = meta[5, 0]
    lead = meta[5, 1]
    tiles = (live_rows + TILE - 1) // TILE

    def source_base(h):
        return pl.multiple_of(lax.rem(me - h + splits, splits) * width, width)

    env_copies = [pltpu.make_async_copy(own_hbm, env.at[pl.ds(source_base(0), width)], env_sem.at[0])] + [
        pltpu.make_async_copy(others_e[h - 1], env.at[pl.ds(source_base(h), width)], env_sem.at[h])
        for h in range(1, splits)
    ]

    def some(k):
        return (meta[2, k] >= 0) & (meta[1, k] > me * width)

    def small_wanted(k):
        return some(k) & (meta[1, k] <= width)

    def wide_wanted(k):
        return some(k) & ((k < first) | (meta[1, k] > width))

    def crossing(k):
        return some(k) & (meta[1, k] > width)

    def mine_copy(k):
        return pltpu.make_async_copy(t_hbm.at[meta[2, k]], mine.at[k % 2], mine_sem.at[k % 2])

    def begin(k, wanted):
        @pl.when(wanted(k))
        def _():
            mine_copy(k).start()

    def small_copy(k):
        return pltpu.make_async_copy(small.at[k - first], small_hbm.at[k - first], small_sem.at[k - first])

    def wide_copy(k, act):
        @pl.when(k < first)
        def _():
            act(pltpu.make_async_copy(wide.at[k], low_hbm.at[jnp.minimum(k, first - 1)], wide_sem.at[k]))

        @pl.when(k >= first)
        def _():
            act(pltpu.make_async_copy(wide.at[k], high_hbm.at[jnp.maximum(k - first, 0)], wide_sem.at[k]))

    def product_copy(k):
        return pltpu.make_async_copy(product.at[meta[3, k]], products_hbm.at[meta[3, k]], product_sem.at[meta[3, k]])

    def multiply(k, p):
        mine_copy(k).wait()
        mask(mine.at[k % 2], meta[1, k] - me * width, live_rows, width)

        def step(b, carry):
            base = pl.multiple_of(b * TILE, TILE)
            value = jnp.dot(env[pl.ds(base, TILE), :], mine[k % 2], preferred_element_type=jnp.float32)
            product[p, pl.ds(base, TILE), :] = value.astype(jnp.bfloat16)
            return carry

        def clear(b, carry):
            product[p, pl.ds(pl.multiple_of(b * TILE, TILE), TILE), :] = jnp.zeros((TILE, width), jnp.bfloat16)
            return carry

        lax.fori_loop(0, tiles, step, 0)
        lax.fori_loop(tiles, span // TILE, clear, 0)

    for copy in env_copies:
        copy.start()
    begin(first, small_wanted)
    for copy in env_copies:
        copy.wait()

    def one_small(k, carry):
        @pl.when(k + 1 < sectors)
        def _():
            begin(k + 1, small_wanted)

        @pl.when(jnp.logical_not(small_wanted(k)))
        def _():
            small[k - first] = jnp.zeros((width, width), jnp.bfloat16)

        @pl.when(small_wanted(k))
        def _():
            multiply(k, states)
            half(flat_store(small.at[k - first], 0), mine.at[k % 2], product.at[states], width)

        small_copy(k).start()
        return carry

    lax.fori_loop(first, sectors, one_small, 0)
    begin(0, wide_wanted)

    def one_wide(k, carry):
        size = meta[1, k]
        p = meta[3, k]

        @pl.when(k + 1 < lead)
        def _():
            begin(k + 1, wide_wanted)

        @pl.when(jnp.logical_not(wide_wanted(k)))
        def _():
            wide[k] = jnp.zeros(wide.shape[1:], jnp.bfloat16)

        @pl.when(wide_wanted(k))
        def _():
            multiply(k, p)
            half(flat_store(wide.at[k], me * width), mine.at[k % 2], product.at[p], width)
            for h in range(1, splits):
                @pl.when(jnp.logical_not((size > width) & (size > source_base(h))))
                def _():
                    wide[k, pl.ds(source_base(h), width), :] = jnp.zeros((width, width), jnp.bfloat16)

        wide_copy(k, lambda copy: copy.start())

        @pl.when(crossing(k))
        def _():
            product_copy(k).start()

        return carry

    lax.fori_loop(0, lead, one_wide, 0)

    def end_small(k, carry):
        small_copy(k).wait()
        return carry

    def end_wide(k, carry):
        wide_copy(k, lambda copy: copy.wait())

        @pl.when(crossing(k))
        def _():
            product_copy(k).wait()

        return carry

    lax.fori_loop(first, sectors, end_small, 0)
    lax.fori_loop(0, lead, end_wide, 0)


def mask(ref, cols, live_rows, width):
    def step(b, carry):
        base = pl.multiple_of(b * TILE, TILE)
        rows_here = lax.broadcasted_iota(jnp.int32, (TILE, width), 0) + base
        cols_here = lax.broadcasted_iota(jnp.int32, (TILE, width), 1)
        keep = (rows_here < live_rows) & (cols_here < cols)
        ref[pl.ds(base, TILE), :] = jnp.where(keep, ref[pl.ds(base, TILE), :], jnp.zeros((), jnp.bfloat16))
        return carry

    lax.fori_loop(0, ref.shape[0] // TILE, step, 0)


def flat_store(ref, row_base):
    def store(base, value):
        ref[pl.ds(pl.multiple_of(row_base + base, TILE), TILE), :] = value

    return store


def half(store, factor, product, width):
    def step(j, carry):
        base = pl.multiple_of(j * TILE, TILE)
        value = lax.dot_general(
            factor[:, pl.ds(base, TILE)], product[...], (((0,), (0,)), ((), ())), preferred_element_type=jnp.float32
        )
        store(base, value.astype(jnp.bfloat16))
        return carry

    lax.fori_loop(0, width // TILE, step, 0)


def other_kernel(first, states, span, width, splits, *refs):
    meta, products_hbm = refs[0], refs[3]
    others_t = refs[4 : 4 + (splits - 1) * states]
    low_hbm, high_hbm, theirs, product, result, theirs_sem, product_sem, out_sem = refs[4 + len(others_t) :]
    me = lax.axis_index("split")
    live_rows = meta[5, 0]
    stop = meta[5, 1]

    def source_base(h):
        return pl.multiple_of(lax.rem(me - h + splits, splits) * width, width)

    def crossing(k):
        return (meta[2, k] >= 0) & (meta[1, k] > me * width) & (meta[1, k] > width)

    def wanted(k, h):
        return crossing(k) & (meta[1, k] > source_base(h))

    def product_copy(k):
        return pltpu.make_async_copy(products_hbm.at[meta[3, k]], product.at[k % 2], product_sem.at[k % 2])

    def theirs_copy(k, h, slot):
        return pltpu.make_async_copy(others_t[(h - 1) * states + slot], theirs.at[k % 2, h - 1], theirs_sem.at[k % 2, h - 1])

    def out_copy(k, h, act):
        rows = pl.ds(source_base(h), width)

        @pl.when(k < first)
        def _():
            to = low_hbm.at[jnp.minimum(k, first - 1), rows]
            act(pltpu.make_async_copy(result.at[k, h - 1], to, out_sem.at[k, h - 1]))

        @pl.when(k >= first)
        def _():
            to = high_hbm.at[jnp.maximum(k - first, 0), rows]
            act(pltpu.make_async_copy(result.at[k, h - 1], to, out_sem.at[k, h - 1]))

    def begin(k):
        @pl.when(crossing(k))
        def _():
            product_copy(k).start()
            for slot in range(states):
                @pl.when(meta[3, k] == slot)
                def _():
                    for h in range(1, splits):
                        theirs_copy(k, h, slot).start()

    begin(0)

    def one(k, carry):
        @pl.when(k + 1 < stop)
        def _():
            begin(k + 1)

        @pl.when(crossing(k))
        def _():
            product_copy(k).wait()
            for h in range(1, splits):
                theirs_copy(k, h, 0).wait()
            for h in range(1, splits):
                @pl.when(wanted(k, h))
                def _():
                    mask(theirs.at[k % 2, h - 1], meta[1, k] - source_base(h), live_rows, width)
                    half(flat_store(result.at[k, h - 1], 0), theirs.at[k % 2, h - 1], product.at[k % 2], width)
                    out_copy(k, h, lambda copy: copy.start())

        return carry

    lax.fori_loop(0, stop, one, 0)

    def finish(k, carry):
        for h in range(1, splits):
            @pl.when(wanted(k, h))
            def _():
                out_copy(k, h, lambda copy: copy.wait())
        return carry

    lax.fori_loop(0, stop, finish, 0)


def finish_kernel(sectors, first, width, pieces, meta, low_ref, high_ref, *refs):
    small, out_ref = refs[:pieces], refs[pieces]
    rows = out_ref.shape[1] // pieces
    for r in range(sectors):
        rank = meta[0, r]
        above = jnp.maximum(rank - first, 0)
        large = meta[1, rank] > width

        @pl.when(rank < first)
        def _():
            out_ref[r] = low_ref[jnp.minimum(rank, first - 1)].astype(jnp.float32)

        @pl.when((rank >= first) & large)
        def _():
            out_ref[r] = high_ref[above].astype(jnp.float32)

        @pl.when((rank >= first) & jnp.logical_not(large))
        def _():
            for p in range(pieces):
                out_ref[r, p * rows : (p + 1) * rows, :] = small[p][above].astype(jnp.float32)


def blank_kernel(out_ref):
    pass


ANY = pl.BlockSpec(memory_space=pl.ANY)
HBM = pl.BlockSpec(memory_space=pltpu.HBM)
SMEM = pl.BlockSpec(memory_space=pltpu.SMEM)
VMEM = pl.BlockSpec(memory_space=pltpu.VMEM)
PARAMS = pltpu.CompilerParams(vmem_limit_bytes=62 * 1024 * 1024)


def own_terms(first, sectors, meta, tensor, env, other_env, splits):
    states, span, width = tensor.shape
    small = jax.ShapeDtypeStruct((sectors - first, width, width), jnp.bfloat16)
    low = jax.ShapeDtypeStruct((first, span, width), jnp.bfloat16)
    high = jax.ShapeDtypeStruct((sectors - first, span, width), jnp.bfloat16)
    products = jax.ShapeDtypeStruct((states, span, width), jnp.bfloat16)
    return pl.pallas_call(
        functools.partial(own_kernel, first, sectors, states, span, width, splits),
        out_shape=[small, low, high, products],
        in_specs=[SMEM] + [ANY] * (2 + len(other_env)),
        out_specs=[HBM] * 4,
        scratch_shapes=[
            pltpu.VMEM((span, span), jnp.bfloat16),
            pltpu.VMEM((2, span, width), jnp.bfloat16),
            pltpu.VMEM((states + 1, span, width), jnp.bfloat16),
            pltpu.VMEM(small.shape, jnp.bfloat16),
            pltpu.VMEM((sectors, span, width), jnp.bfloat16),
            pltpu.SemaphoreType.DMA((splits,)),
            pltpu.SemaphoreType.DMA((2,)),
            pltpu.SemaphoreType.DMA((sectors - first,)),
            pltpu.SemaphoreType.DMA((sectors,)),
            pltpu.SemaphoreType.DMA((states + 1,)),
        ],
        compiler_params=PARAMS,
        cost_estimate=pl.CostEstimate(
            flops=4 * states * span * span * width, bytes_accessed=8 * span * width, transcendentals=0
        ),
    )(meta, tensor, env, *other_env)


def other_terms(meta, low, high, products, other_tensor, states, splits):
    first, span, width = low.shape
    sectors = first + high.shape[0]
    others = max(splits - 1, 1)
    return pl.pallas_call(
        functools.partial(other_kernel, first, states, span, width, splits),
        out_shape=[jax.ShapeDtypeStruct(a.shape, jnp.bfloat16) for a in (low, high)],
        in_specs=[SMEM, HBM, HBM, ANY] + [ANY] * len(other_tensor),
        out_specs=[HBM, HBM],
        input_output_aliases={1: 0, 2: 1},
        scratch_shapes=[
            pltpu.VMEM((2, others, span, width), jnp.bfloat16),
            pltpu.VMEM((2, span, width), jnp.bfloat16),
            pltpu.VMEM((sectors, others, width, width), jnp.bfloat16),
            pltpu.SemaphoreType.DMA((2, others)),
            pltpu.SemaphoreType.DMA((2,)),
            pltpu.SemaphoreType.DMA((sectors, others)),
        ],
        compiler_params=PARAMS,
    )(meta, low, high, products, *other_tensor)


def blank(shape):
    return pl.pallas_call(
        blank_kernel, out_shape=jax.ShapeDtypeStruct(shape, jnp.bfloat16), out_specs=HBM, compiler_params=PARAMS
    )()


def body(left_env, site_tensor, left_sizes, right_sizes, targets):
    splits = lax.axis_size("split")
    lanes = lax.axis_size("charge")
    tensor, env = site_tensor[0], left_env[0]
    states, span, width = tensor.shape
    sectors = right_sizes.shape[0]
    first = sectors // 2
    leads = sorted({first, max(sectors * 5 // 8, first), sectors})
    shifts = [[(y, (y + h) % splits) for y in range(splits)] for h in range(1, splits)]
    depths = max(span // TILE // (splits - 1), 1) if splits > 1 else 1
    grain = span // depths
    blocks = (left_sizes[0] + grain - 1) // grain

    groups = lax.axis_size("groups")
    other_sizes = [
        lax.ppermute(right_sizes, "groups", [(g, (g + h) % groups) for g in range(groups)]) for h in range(1, groups)
    ]

    def send_env(v):
        rows = min(v * grain, width)
        senders = -(-v * grain // width)

        def branch(block):
            piece = block[:rows, : v * grain]
            got = [lax.ppermute(piece, "split", [p for p in pairs if p[0] < senders]) for pairs in shifts]
            return tuple(jnp.pad(g, ((0, width - rows), (0, span - v * grain))) for g in got)

        return branch

    other_env = lax.switch(blocks - 1, [send_env(v) for v in range(1, depths + 1)], env)

    meta = pl.pallas_call(
        functools.partial(meta_kernel, sectors, states, width, depths, grain, leads),
        out_shape=jax.ShapeDtypeStruct((6, max(sectors, 8)), jnp.int32),
        in_specs=[SMEM] * (3 + len(other_sizes)),
        out_specs=SMEM,
    )(left_sizes, targets, right_sizes, *other_sizes)

    piece = lax.dynamic_slice(tensor, (meta[4, 0], 0, 0), (1, span, width))[0]
    piece, other_env = lax.optimization_barrier((piece, other_env))
    slot_first = [lax.ppermute(piece, "split", pairs) for pairs in shifts]

    small, low, high, products = own_terms(first, sectors, meta, tensor, env, other_env, splits)
    small, low, tensor, slot_first = lax.optimization_barrier((small, low, tensor, slot_first))
    small_sum = lax.psum_scatter(small, "charge", scatter_dimension=1, tiled=True)

    def send_tensor(used, v):
        def branch(block, meta):
            got = []
            for pairs in shifts:
                for i in range(1, states):
                    if i >= used:
                        got.append(blank((span, width)))
                        continue
                    piece = lax.dynamic_slice(block, (meta[4, i], 0, 0), (1, v * grain, width))[0]
                    got.append(jnp.pad(lax.ppermute(piece, "split", pairs), ((0, span - v * grain), (0, 0))))
            return tuple(got)

        return branch

    branches = [send_tensor(1, 1)] + [send_tensor(u, v) for u in range(2, states + 1) for v in range(1, depths + 1)]
    more = lax.switch(meta[5, 3], branches, tensor, meta)
    other_tensor = []
    for h in range(splits - 1):
        other_tensor += [slot_first[h], *more[h * (states - 1) : (h + 1) * (states - 1)]]
    low, high = other_terms(meta, low, high, products, other_tensor, states, splits)
    share = span // lanes

    def scatter(lead):
        def branch(low, high, small_sum, meta):
            low_sum = lax.psum_scatter(low, "charge", scatter_dimension=1, tiled=True)
            if lead == first:
                high_sum = blank((sectors - first, share, width))
            else:
                high_sum = lax.psum_scatter(high[: lead - first], "charge", scatter_dimension=1, tiled=True)
                high_sum = jnp.pad(high_sum, ((0, sectors - lead), (0, 0), (0, 0)))
            owned = [
                lax.ppermute(small_sum, "charge", [(j, j // splits) for j in range(lanes) if j % splits == p])
                for p in range(splits)
            ]
            return pl.pallas_call(
                functools.partial(finish_kernel, sectors, first, width, splits),
                out_shape=jax.ShapeDtypeStruct((sectors, share, width), jnp.float32),
                in_specs=[SMEM] + [VMEM] * (2 + splits),
                out_specs=VMEM,
                compiler_params=PARAMS,
            )(meta, low_sum, high_sum, *owned)

        return branch

    return lax.switch(meta[5, 2], [scatter(lead) for lead in leads], low, high, small_sum, meta)


def solution(mesh):
    in_specs = (
        P(("groups", "charge"), "split", None),
        P(("groups", "charge"), None, None, "split"),
        P(("groups", "charge")),
        P("groups"),
        P(("groups", "charge"), None),
    )
    out_specs = P("groups", "charge", "split")
    return jax.shard_map(body, mesh=mesh, in_specs=in_specs, out_specs=out_specs, check_vma=False)
```

```python
import functools

import jax
import jax.numpy as jnp
from jax import lax
from jax.experimental import pallas as pl
from jax.experimental.pallas import tpu as pltpu
from jax.sharding import PartitionSpec as P

TILE = 256


def meta_kernel(sectors, states, width, depths, grain, leads, left_ref, target_ref, right_ref, *refs):
    others, out_ref = refs[:-1], refs[-1]

    def rank_sector(r, carry):
        size = right_ref[r]

        def count(other, total):
            bigger = (right_ref[other] > size) | ((right_ref[other] == size) & (other < r))
            return total + bigger.astype(jnp.int32)

        rank = lax.fori_loop(0, sectors, count, jnp.int32(0), unroll=True)
        out_ref[0, r] = rank
        out_ref[1, rank] = size
        out_ref[2, rank] = jnp.int32(-1)
        out_ref[3, rank] = jnp.int32(states)
        out_ref[4, r] = jnp.int32(0)
        out_ref[5, r] = jnp.int32(0)
        return carry

    lax.fori_loop(0, sectors, rank_sector, 0)
    for s in range(states):
        out_ref[2, out_ref[0, target_ref[0, s]]] = jnp.int32(s)

    def place(k, used):
        state = out_ref[2, k]
        wanted = (state >= 0) & (out_ref[1, k] > width)

        @pl.when(wanted)
        def _():
            out_ref[3, k] = used
            out_ref[4, used] = state

        return used + wanted.astype(jnp.int32)

    used = lax.fori_loop(0, sectors, place, jnp.int32(0))
    most = jnp.int32(0)
    for ref in (right_ref,) + others:
        def wide(r, total, ref=ref):
            return total + (ref[r] > width).astype(jnp.int32)

        most = jnp.maximum(most, lax.fori_loop(0, sectors, wide, jnp.int32(0), unroll=True))
    lead, choice = jnp.int32(leads[-1]), jnp.int32(0)
    for e in reversed(leads[:-1]):
        lead = jnp.where(most <= e, jnp.int32(e), lead)
    for e in leads[:-1]:
        choice = choice + (most > e).astype(jnp.int32)
    depth = (left_ref[0] + grain - 1) // grain
    out_ref[5, 0] = left_ref[0]
    out_ref[5, 1] = lead
    out_ref[5, 2] = choice
    out_ref[5, 3] = jnp.where(used <= 1, 0, 1 + (used - 2) * depths + depth - 1)


def own_kernel(leading, first, sectors, states, span, width, splits, *refs):
    meta, t_hbm, own_hbm = refs[:3]
    others_e = refs[3 : 3 + splits - 1]
    at = 2 + splits
    if leading:
        low_hbm, high_hbm, products_hbm, env, mine, product, wide, env_sem, mine_sem, wide_sem, product_sem = refs[at:]
    else:
        small_hbm, env, mine, product, small, env_sem, mine_sem, small_sem = refs[at:]
    me = lax.axis_index("split")
    live_rows = meta[5, 0]
    lead = meta[5, 1]
    tiles = (live_rows + TILE - 1) // TILE

    def source_base(h):
        return pl.multiple_of(lax.rem(me - h + splits, splits) * width, width)

    env_copies = [pltpu.make_async_copy(own_hbm, env.at[pl.ds(source_base(0), width)], env_sem.at[0])] + [
        pltpu.make_async_copy(others_e[h - 1], env.at[pl.ds(source_base(h), width)], env_sem.at[h])
        for h in range(1, splits)
    ]

    def some(k):
        return (meta[2, k] >= 0) & (meta[1, k] > me * width)

    def small_wanted(k):
        return some(k) & (meta[1, k] <= width)

    def wide_wanted(k):
        return some(k) & ((k < first) | (meta[1, k] > width))

    def crossing(k):
        return some(k) & (meta[1, k] > width)

    def mine_copy(k):
        return pltpu.make_async_copy(t_hbm.at[meta[2, k]], mine.at[k % 2], mine_sem.at[k % 2])

    def begin(k, wanted):
        @pl.when(wanted(k))
        def _():
            mine_copy(k).start()

    def small_copy(k):
        return pltpu.make_async_copy(small.at[k - first], small_hbm.at[k - first], small_sem.at[k - first])

    def wide_copy(k, act):
        @pl.when(k < first)
        def _():
            act(pltpu.make_async_copy(wide.at[k], low_hbm.at[jnp.minimum(k, first - 1)], wide_sem.at[k]))

        @pl.when(k >= first)
        def _():
            act(pltpu.make_async_copy(wide.at[k], high_hbm.at[jnp.maximum(k - first, 0)], wide_sem.at[k]))

    def product_copy(k):
        return pltpu.make_async_copy(product.at[meta[3, k]], products_hbm.at[meta[3, k]], product_sem.at[meta[3, k]])

    def multiply(k, p):
        mine_copy(k).wait()
        mask(mine.at[k % 2], meta[1, k] - me * width, live_rows, width)

        def step(b, carry):
            base = pl.multiple_of(b * TILE, TILE)
            value = jnp.dot(env[pl.ds(base, TILE), :], mine[k % 2], preferred_element_type=jnp.float32)
            product[p, pl.ds(base, TILE), :] = value.astype(jnp.bfloat16)
            return carry

        def clear(b, carry):
            product[p, pl.ds(pl.multiple_of(b * TILE, TILE), TILE), :] = jnp.zeros((TILE, width), jnp.bfloat16)
            return carry

        lax.fori_loop(0, tiles, step, 0)
        lax.fori_loop(tiles, span // TILE, clear, 0)

    for copy in env_copies:
        copy.start()
    if leading:
        begin(0, wide_wanted)
    else:
        begin(first, small_wanted)
    for copy in env_copies:
        copy.wait()

    def one_small(k, carry):
        @pl.when(k + 1 < sectors)
        def _():
            begin(k + 1, small_wanted)

        @pl.when(jnp.logical_not(small_wanted(k)))
        def _():
            small[k - first] = jnp.zeros((width, width), jnp.bfloat16)

        @pl.when(small_wanted(k))
        def _():
            multiply(k, 0)
            half(flat_store(small.at[k - first], 0), mine.at[k % 2], product.at[0], width)

        small_copy(k).start()
        return carry

    def one_wide(k, carry):
        size = meta[1, k]
        p = meta[3, k]

        @pl.when(k + 1 < lead)
        def _():
            begin(k + 1, wide_wanted)

        @pl.when(jnp.logical_not(wide_wanted(k)))
        def _():
            wide[k] = jnp.zeros(wide.shape[1:], jnp.bfloat16)

        @pl.when(wide_wanted(k))
        def _():
            multiply(k, p)
            half(flat_store(wide.at[k], me * width), mine.at[k % 2], product.at[p], width)
            for h in range(1, splits):
                @pl.when(jnp.logical_not((size > width) & (size > source_base(h))))
                def _():
                    wide[k, pl.ds(source_base(h), width), :] = jnp.zeros((width, width), jnp.bfloat16)

        wide_copy(k, lambda copy: copy.start())

        @pl.when(crossing(k))
        def _():
            product_copy(k).start()

        return carry

    def end_small(k, carry):
        small_copy(k).wait()
        return carry

    def end_wide(k, carry):
        wide_copy(k, lambda copy: copy.wait())

        @pl.when(crossing(k))
        def _():
            product_copy(k).wait()

        return carry

    if leading:
        lax.fori_loop(0, lead, one_wide, 0)
        lax.fori_loop(0, lead, end_wide, 0)
    else:
        lax.fori_loop(first, sectors, one_small, 0)
        lax.fori_loop(first, sectors, end_small, 0)


def mask(ref, cols, live_rows, width):
    def step(b, carry):
        base = pl.multiple_of(b * TILE, TILE)
        rows_here = lax.broadcasted_iota(jnp.int32, (TILE, width), 0) + base
        cols_here = lax.broadcasted_iota(jnp.int32, (TILE, width), 1)
        keep = (rows_here < live_rows) & (cols_here < cols)
        ref[pl.ds(base, TILE), :] = jnp.where(keep, ref[pl.ds(base, TILE), :], jnp.zeros((), jnp.bfloat16))
        return carry

    lax.fori_loop(0, ref.shape[0] // TILE, step, 0)


def flat_store(ref, row_base):
    def store(base, value):
        ref[pl.ds(pl.multiple_of(row_base + base, TILE), TILE), :] = value

    return store


def half(store, factor, product, width):
    def step(j, carry):
        base = pl.multiple_of(j * TILE, TILE)
        value = lax.dot_general(
            factor[:, pl.ds(base, TILE)], product[...], (((0,), (0,)), ((), ())), preferred_element_type=jnp.float32
        )
        store(base, value.astype(jnp.bfloat16))
        return carry

    lax.fori_loop(0, width // TILE, step, 0)


def other_kernel(first, states, span, width, splits, *refs):
    meta, products_hbm = refs[0], refs[3]
    others_t = refs[4 : 4 + (splits - 1) * states]
    low_hbm, high_hbm, theirs, product, result, theirs_sem, product_sem, out_sem = refs[4 + len(others_t) :]
    me = lax.axis_index("split")
    live_rows = meta[5, 0]
    stop = meta[5, 1]

    def source_base(h):
        return pl.multiple_of(lax.rem(me - h + splits, splits) * width, width)

    def crossing(k):
        return (meta[2, k] >= 0) & (meta[1, k] > me * width) & (meta[1, k] > width)

    def wanted(k, h):
        return crossing(k) & (meta[1, k] > source_base(h))

    def product_copy(k):
        return pltpu.make_async_copy(products_hbm.at[meta[3, k]], product.at[k % 2], product_sem.at[k % 2])

    def theirs_copy(k, h, slot):
        return pltpu.make_async_copy(others_t[(h - 1) * states + slot], theirs.at[k % 2, h - 1], theirs_sem.at[k % 2, h - 1])

    def out_copy(k, h, act):
        rows = pl.ds(source_base(h), width)

        @pl.when(k < first)
        def _():
            to = low_hbm.at[jnp.minimum(k, first - 1), rows]
            act(pltpu.make_async_copy(result.at[k, h - 1], to, out_sem.at[k, h - 1]))

        @pl.when(k >= first)
        def _():
            to = high_hbm.at[jnp.maximum(k - first, 0), rows]
            act(pltpu.make_async_copy(result.at[k, h - 1], to, out_sem.at[k, h - 1]))

    def begin(k):
        @pl.when(crossing(k))
        def _():
            product_copy(k).start()
            for slot in range(states):
                @pl.when(meta[3, k] == slot)
                def _():
                    for h in range(1, splits):
                        theirs_copy(k, h, slot).start()

    begin(0)

    def one(k, carry):
        @pl.when(k + 1 < stop)
        def _():
            begin(k + 1)

        @pl.when(crossing(k))
        def _():
            product_copy(k).wait()
            for h in range(1, splits):
                theirs_copy(k, h, 0).wait()
            for h in range(1, splits):
                @pl.when(wanted(k, h))
                def _():
                    mask(theirs.at[k % 2, h - 1], meta[1, k] - source_base(h), live_rows, width)
                    half(flat_store(result.at[k, h - 1], 0), theirs.at[k % 2, h - 1], product.at[k % 2], width)
                    out_copy(k, h, lambda copy: copy.start())

        return carry

    lax.fori_loop(0, stop, one, 0)

    def finish(k, carry):
        for h in range(1, splits):
            @pl.when(wanted(k, h))
            def _():
                out_copy(k, h, lambda copy: copy.wait())
        return carry

    lax.fori_loop(0, stop, finish, 0)


def finish_kernel(sectors, first, width, pieces, meta, low_ref, high_ref, *refs):
    small, out_ref = refs[:pieces], refs[pieces]
    rows = out_ref.shape[1] // pieces
    for r in range(sectors):
        rank = meta[0, r]
        above = jnp.maximum(rank - first, 0)
        large = meta[1, rank] > width

        @pl.when(rank < first)
        def _():
            out_ref[r] = low_ref[jnp.minimum(rank, first - 1)].astype(jnp.float32)

        @pl.when((rank >= first) & large)
        def _():
            out_ref[r] = high_ref[above].astype(jnp.float32)

        @pl.when((rank >= first) & jnp.logical_not(large))
        def _():
            for p in range(pieces):
                out_ref[r, p * rows : (p + 1) * rows, :] = small[p][above].astype(jnp.float32)


def blank_kernel(out_ref):
    pass


ANY = pl.BlockSpec(memory_space=pl.ANY)
HBM = pl.BlockSpec(memory_space=pltpu.HBM)
SMEM = pl.BlockSpec(memory_space=pltpu.SMEM)
VMEM = pl.BlockSpec(memory_space=pltpu.VMEM)
PARAMS = pltpu.CompilerParams(vmem_limit_bytes=62 * 1024 * 1024)


def own_terms(leading, first, sectors, meta, tensor, env, other_env, splits):
    states, span, width = tensor.shape
    small = jax.ShapeDtypeStruct((sectors - first, width, width), jnp.bfloat16)
    low = jax.ShapeDtypeStruct((first, span, width), jnp.bfloat16)
    high = jax.ShapeDtypeStruct((sectors - first, span, width), jnp.bfloat16)
    products = jax.ShapeDtypeStruct((states, span, width), jnp.bfloat16)
    sems = [pltpu.SemaphoreType.DMA((splits,)), pltpu.SemaphoreType.DMA((2,))]
    if leading:
        outs = [low, high, products]
        held = (sectors, span, width)
        sems += [pltpu.SemaphoreType.DMA((sectors,)), pltpu.SemaphoreType.DMA((states + 1,))]
    else:
        outs = [small]
        held = small.shape
        sems += [pltpu.SemaphoreType.DMA((sectors - first,))]
    return pl.pallas_call(
        functools.partial(own_kernel, leading, first, sectors, states, span, width, splits),
        out_shape=outs,
        in_specs=[SMEM] + [ANY] * (2 + len(other_env)),
        out_specs=[HBM] * len(outs),
        scratch_shapes=[
            pltpu.VMEM((span, span), jnp.bfloat16),
            pltpu.VMEM((2, span, width), jnp.bfloat16),
            pltpu.VMEM((states + 1 if leading else 1, span, width), jnp.bfloat16),
            pltpu.VMEM(held, jnp.bfloat16),
        ]
        + sems,
        compiler_params=PARAMS,
        cost_estimate=pl.CostEstimate(
            flops=4 * states * span * span * width, bytes_accessed=8 * span * width, transcendentals=0
        ),
    )(meta, tensor, env, *other_env)


def other_terms(meta, low, high, products, other_tensor, states, splits):
    first, span, width = low.shape
    sectors = first + high.shape[0]
    others = max(splits - 1, 1)
    return pl.pallas_call(
        functools.partial(other_kernel, first, states, span, width, splits),
        out_shape=[jax.ShapeDtypeStruct(a.shape, jnp.bfloat16) for a in (low, high)],
        in_specs=[SMEM, HBM, HBM, ANY] + [ANY] * len(other_tensor),
        out_specs=[HBM, HBM],
        input_output_aliases={1: 0, 2: 1},
        scratch_shapes=[
            pltpu.VMEM((2, others, span, width), jnp.bfloat16),
            pltpu.VMEM((2, span, width), jnp.bfloat16),
            pltpu.VMEM((sectors, others, width, width), jnp.bfloat16),
            pltpu.SemaphoreType.DMA((2, others)),
            pltpu.SemaphoreType.DMA((2,)),
            pltpu.SemaphoreType.DMA((sectors, others)),
        ],
        compiler_params=PARAMS,
    )(meta, low, high, products, *other_tensor)


def blank(shape):
    return pl.pallas_call(
        blank_kernel, out_shape=jax.ShapeDtypeStruct(shape, jnp.bfloat16), out_specs=HBM, compiler_params=PARAMS
    )()


def body(left_env, site_tensor, left_sizes, right_sizes, targets):
    splits = lax.axis_size("split")
    lanes = lax.axis_size("charge")
    tensor, env = site_tensor[0], left_env[0]
    states, span, width = tensor.shape
    sectors = right_sizes.shape[0]
    first = sectors // 2
    leads = sorted({first, max(sectors * 5 // 8, first), sectors})
    shifts = [[(y, (y + h) % splits) for y in range(splits)] for h in range(1, splits)]
    depths = max(span // TILE // (splits - 1), 1) if splits > 1 else 1
    grain = span // depths
    blocks = (left_sizes[0] + grain - 1) // grain

    groups = lax.axis_size("groups")
    other_sizes = [
        lax.ppermute(right_sizes, "groups", [(g, (g + h) % groups) for g in range(groups)]) for h in range(1, groups)
    ]

    def send_env(v):
        rows = min(v * grain, width)
        senders = -(-v * grain // width)

        def branch(block):
            piece = block[:rows, : v * grain]
            got = [lax.ppermute(piece, "split", [p for p in pairs if p[0] < senders]) for pairs in shifts]
            return tuple(jnp.pad(g, ((0, width - rows), (0, span - v * grain))) for g in got)

        return branch

    other_env = lax.switch(blocks - 1, [send_env(v) for v in range(1, depths + 1)], env)

    meta = pl.pallas_call(
        functools.partial(meta_kernel, sectors, states, width, depths, grain, leads),
        out_shape=jax.ShapeDtypeStruct((6, max(sectors, 8)), jnp.int32),
        in_specs=[SMEM] * (3 + len(other_sizes)),
        out_specs=SMEM,
    )(left_sizes, targets, right_sizes, *other_sizes)

    piece = lax.dynamic_slice(tensor, (meta[4, 0], 0, 0), (1, span, width))[0]
    slot_first = [lax.ppermute(piece, "split", pairs) for pairs in shifts]

    (small,) = own_terms(False, first, sectors, meta, tensor, env, other_env, splits)
    small, env = lax.optimization_barrier((small, env))
    small_sum = lax.psum_scatter(small, "charge", scatter_dimension=1, tiled=True)
    low, high, products = own_terms(True, first, sectors, meta, tensor, env, other_env, splits)
    low, tensor = lax.optimization_barrier((low, tensor))

    def send_tensor(used, v):
        def branch(block, meta):
            got = []
            for pairs in shifts:
                for i in range(1, states):
                    if i >= used:
                        got.append(blank((span, width)))
                        continue
                    piece = lax.dynamic_slice(block, (meta[4, i], 0, 0), (1, v * grain, width))[0]
                    got.append(jnp.pad(lax.ppermute(piece, "split", pairs), ((0, span - v * grain), (0, 0))))
            return tuple(got)

        return branch

    branches = [send_tensor(1, 1)] + [send_tensor(u, v) for u in range(2, states + 1) for v in range(1, depths + 1)]
    more = lax.switch(meta[5, 3], branches, tensor, meta)
    other_tensor = []
    for h in range(splits - 1):
        other_tensor += [slot_first[h], *more[h * (states - 1) : (h + 1) * (states - 1)]]
    low, high = other_terms(meta, low, high, products, other_tensor, states, splits)
    share = span // lanes

    def scatter(lead):
        def branch(low, high, small_sum, meta):
            low_sum = lax.psum_scatter(low, "charge", scatter_dimension=1, tiled=True)
            if lead == first:
                high_sum = blank((sectors - first, share, width))
            else:
                high_sum = lax.psum_scatter(high[: lead - first], "charge", scatter_dimension=1, tiled=True)
                high_sum = jnp.pad(high_sum, ((0, sectors - lead), (0, 0), (0, 0)))
            owned = [
                lax.ppermute(small_sum, "charge", [(j, j // splits) for j in range(lanes) if j % splits == p])
                for p in range(splits)
            ]
            return pl.pallas_call(
                functools.partial(finish_kernel, sectors, first, width, splits),
                out_shape=jax.ShapeDtypeStruct((sectors, share, width), jnp.float32),
                in_specs=[SMEM] + [VMEM] * (2 + splits),
                out_specs=VMEM,
                compiler_params=PARAMS,
            )(meta, low_sum, high_sum, *owned)

        return branch

    return lax.switch(meta[5, 2], [scatter(lead) for lead in leads], low, high, small_sum, meta)


def solution(mesh):
    in_specs = (
        P(("groups", "charge"), "split", None),
        P(("groups", "charge"), None, None, "split"),
        P(("groups", "charge")),
        P("groups"),
        P(("groups", "charge"), None),
    )
    out_specs = P("groups", "charge", "split")
    return jax.shard_map(body, mesh=mesh, in_specs=in_specs, out_specs=out_specs, check_vma=False)
```

```python
import functools

import jax
import jax.numpy as jnp
from jax import lax
from jax.experimental import pallas as pl
from jax.experimental.pallas import tpu as pltpu
from jax.sharding import PartitionSpec as P

TILE = 256


def meta_kernel(sectors, states, width, depths, grain, leads, left_ref, target_ref, right_ref, *refs):
    others, out_ref = refs[:-1], refs[-1]

    def rank_sector(r, carry):
        size = right_ref[r]

        def count(other, total):
            bigger = (right_ref[other] > size) | ((right_ref[other] == size) & (other < r))
            return total + bigger.astype(jnp.int32)

        rank = lax.fori_loop(0, sectors, count, jnp.int32(0), unroll=True)
        out_ref[0, r] = rank
        out_ref[1, rank] = size
        out_ref[2, rank] = jnp.int32(-1)
        out_ref[3, rank] = jnp.int32(states)
        out_ref[4, r] = jnp.int32(0)
        out_ref[5, r] = jnp.int32(0)
        return carry

    lax.fori_loop(0, sectors, rank_sector, 0)
    for s in range(states):
        out_ref[2, out_ref[0, target_ref[0, s]]] = jnp.int32(s)

    def place(k, used):
        state = out_ref[2, k]
        wanted = (state >= 0) & (out_ref[1, k] > width)

        @pl.when(wanted)
        def _():
            out_ref[3, k] = used
            out_ref[4, used] = state

        return used + wanted.astype(jnp.int32)

    used = lax.fori_loop(0, sectors, place, jnp.int32(0))
    most = jnp.int32(0)
    for ref in (right_ref,) + others:
        def wide(r, total, ref=ref):
            return total + (ref[r] > width).astype(jnp.int32)

        most = jnp.maximum(most, lax.fori_loop(0, sectors, wide, jnp.int32(0), unroll=True))
    lead, choice = jnp.int32(leads[-1]), jnp.int32(0)
    for e in reversed(leads[:-1]):
        lead = jnp.where(most <= e, jnp.int32(e), lead)
    for e in leads[:-1]:
        choice = choice + (most > e).astype(jnp.int32)
    depth = (left_ref[0] + grain - 1) // grain
    out_ref[5, 0] = left_ref[0]
    out_ref[5, 1] = lead
    out_ref[5, 2] = choice
    out_ref[5, 3] = jnp.where(used <= 1, 0, 1 + (used - 2) * depths + depth - 1)


def own_kernel(leading, first, sectors, states, span, width, splits, *refs):
    meta, t_hbm, own_hbm = refs[:3]
    others_e = refs[3 : 3 + splits - 1]
    at = 2 + splits
    if leading:
        low_hbm, high_hbm, products_hbm, env, mine, product, wide, env_sem, mine_sem, wide_sem, product_sem = refs[at:]
    else:
        small_hbm, env, mine, product, small, env_sem, mine_sem, small_sem = refs[at:]
    me = lax.axis_index("split")
    live_rows = meta[5, 0]
    lead = meta[5, 1]
    tiles = (live_rows + TILE - 1) // TILE

    def source_base(h):
        return pl.multiple_of(lax.rem(me - h + splits, splits) * width, width)

    env_copies = [pltpu.make_async_copy(own_hbm, env.at[pl.ds(source_base(0), width)], env_sem.at[0])] + [
        pltpu.make_async_copy(others_e[h - 1], env.at[pl.ds(source_base(h), width)], env_sem.at[h])
        for h in range(1, splits)
    ]

    def some(k):
        return (meta[2, k] >= 0) & (meta[1, k] > me * width)

    def small_wanted(k):
        return some(k) & (meta[1, k] <= width)

    def wide_wanted(k):
        return some(k) & ((k < first) | (meta[1, k] > width))

    def crossing(k):
        return some(k) & (meta[1, k] > width)

    def mine_copy(k):
        return pltpu.make_async_copy(t_hbm.at[meta[2, k]], mine.at[k % 2], mine_sem.at[k % 2])

    def begin(k, wanted):
        @pl.when(wanted(k))
        def _():
            mine_copy(k).start()

    def small_copy(k):
        return pltpu.make_async_copy(small.at[k - first], small_hbm.at[k - first], small_sem.at[k - first])

    def wide_copy(k, act):
        @pl.when(k < first)
        def _():
            act(pltpu.make_async_copy(wide.at[k], low_hbm.at[jnp.minimum(k, first - 1)], wide_sem.at[k]))

        @pl.when(k >= first)
        def _():
            act(pltpu.make_async_copy(wide.at[k], high_hbm.at[jnp.maximum(k - first, 0)], wide_sem.at[k]))

    def product_copy(k):
        return pltpu.make_async_copy(product.at[meta[3, k]], products_hbm.at[meta[3, k]], product_sem.at[meta[3, k]])

    def multiply(k, p):
        mine_copy(k).wait()
        mask(mine.at[k % 2], meta[1, k] - me * width, live_rows, width)

        def step(b, carry):
            base = pl.multiple_of(b * TILE, TILE)
            value = jnp.dot(env[pl.ds(base, TILE), :], mine[k % 2], preferred_element_type=jnp.float32)
            product[p, pl.ds(base, TILE), :] = value.astype(jnp.bfloat16)
            return carry

        def clear(b, carry):
            product[p, pl.ds(pl.multiple_of(b * TILE, TILE), TILE), :] = jnp.zeros((TILE, width), jnp.bfloat16)
            return carry

        lax.fori_loop(0, tiles, step, 0)
        lax.fori_loop(tiles, span // TILE, clear, 0)

    for copy in env_copies:
        copy.start()
    if leading:
        begin(0, wide_wanted)
    else:
        begin(first, small_wanted)
    for copy in env_copies:
        copy.wait()

    def one_small(k, carry):
        @pl.when(k + 1 < sectors)
        def _():
            begin(k + 1, small_wanted)

        @pl.when(jnp.logical_not(small_wanted(k)))
        def _():
            small[k - first] = jnp.zeros((width, width), jnp.bfloat16)

        @pl.when(small_wanted(k))
        def _():
            multiply(k, 0)
            half(flat_store(small.at[k - first], 0), mine.at[k % 2], product.at[0], width)

        small_copy(k).start()
        return carry

    def one_wide(k, carry):
        size = meta[1, k]
        p = meta[3, k]

        @pl.when(k + 1 < lead)
        def _():
            begin(k + 1, wide_wanted)

        @pl.when(jnp.logical_not(wide_wanted(k)))
        def _():
            wide[k] = jnp.zeros(wide.shape[1:], jnp.bfloat16)

        @pl.when(wide_wanted(k))
        def _():
            multiply(k, p)
            half(flat_store(wide.at[k], me * width), mine.at[k % 2], product.at[p], width)
            for h in range(1, splits):
                @pl.when(jnp.logical_not((size > width) & (size > source_base(h))))
                def _():
                    wide[k, pl.ds(source_base(h), width), :] = jnp.zeros((width, width), jnp.bfloat16)

        wide_copy(k, lambda copy: copy.start())

        @pl.when(crossing(k))
        def _():
            product_copy(k).start()

        return carry

    def end_small(k, carry):
        small_copy(k).wait()
        return carry

    def end_wide(k, carry):
        wide_copy(k, lambda copy: copy.wait())

        @pl.when(crossing(k))
        def _():
            product_copy(k).wait()

        return carry

    if leading:
        lax.fori_loop(0, lead, one_wide, 0)
        lax.fori_loop(0, lead, end_wide, 0)
    else:
        lax.fori_loop(first, sectors, one_small, 0)
        lax.fori_loop(first, sectors, end_small, 0)


def mask(ref, cols, live_rows, width):
    def step(b, carry):
        base = pl.multiple_of(b * TILE, TILE)
        rows_here = lax.broadcasted_iota(jnp.int32, (TILE, width), 0) + base
        cols_here = lax.broadcasted_iota(jnp.int32, (TILE, width), 1)
        keep = (rows_here < live_rows) & (cols_here < cols)
        ref[pl.ds(base, TILE), :] = jnp.where(keep, ref[pl.ds(base, TILE), :], jnp.zeros((), jnp.bfloat16))
        return carry

    lax.fori_loop(0, ref.shape[0] // TILE, step, 0)


def flat_store(ref, row_base):
    def store(base, value):
        ref[pl.ds(pl.multiple_of(row_base + base, TILE), TILE), :] = value

    return store


def half(store, factor, product, width):
    def step(j, carry):
        base = pl.multiple_of(j * TILE, TILE)
        value = lax.dot_general(
            factor[:, pl.ds(base, TILE)], product[...], (((0,), (0,)), ((), ())), preferred_element_type=jnp.float32
        )
        store(base, value.astype(jnp.bfloat16))
        return carry

    lax.fori_loop(0, width // TILE, step, 0)


def other_kernel(first, states, span, width, splits, *refs):
    meta, products_hbm = refs[0], refs[3]
    others_t = refs[4 : 4 + (splits - 1) * states]
    low_hbm, high_hbm, theirs, product, result, theirs_sem, product_sem, out_sem = refs[4 + len(others_t) :]
    me = lax.axis_index("split")
    live_rows = meta[5, 0]
    stop = meta[5, 1]

    def source_base(h):
        return pl.multiple_of(lax.rem(me - h + splits, splits) * width, width)

    def crossing(k):
        return (meta[2, k] >= 0) & (meta[1, k] > me * width) & (meta[1, k] > width)

    def wanted(k, h):
        return crossing(k) & (meta[1, k] > source_base(h))

    def product_copy(k):
        return pltpu.make_async_copy(products_hbm.at[meta[3, k]], product.at[k % 2], product_sem.at[k % 2])

    def theirs_copy(k, h, slot):
        return pltpu.make_async_copy(others_t[(h - 1) * states + slot], theirs.at[k % 2, h - 1], theirs_sem.at[k % 2, h - 1])

    def out_copy(k, h, act):
        rows = pl.ds(source_base(h), width)

        @pl.when(k < first)
        def _():
            to = low_hbm.at[jnp.minimum(k, first - 1), rows]
            act(pltpu.make_async_copy(result.at[k, h - 1], to, out_sem.at[k, h - 1]))

        @pl.when(k >= first)
        def _():
            to = high_hbm.at[jnp.maximum(k - first, 0), rows]
            act(pltpu.make_async_copy(result.at[k, h - 1], to, out_sem.at[k, h - 1]))

    def begin(k):
        @pl.when(crossing(k))
        def _():
            product_copy(k).start()
            for slot in range(states):
                @pl.when(meta[3, k] == slot)
                def _():
                    for h in range(1, splits):
                        theirs_copy(k, h, slot).start()

    begin(0)

    def one(k, carry):
        @pl.when(k + 1 < stop)
        def _():
            begin(k + 1)

        @pl.when(crossing(k))
        def _():
            product_copy(k).wait()
            for h in range(1, splits):
                theirs_copy(k, h, 0).wait()
            for h in range(1, splits):
                @pl.when(wanted(k, h))
                def _():
                    mask(theirs.at[k % 2, h - 1], meta[1, k] - source_base(h), live_rows, width)
                    half(flat_store(result.at[k, h - 1], 0), theirs.at[k % 2, h - 1], product.at[k % 2], width)
                    out_copy(k, h, lambda copy: copy.start())

        return carry

    lax.fori_loop(0, stop, one, 0)

    def finish(k, carry):
        for h in range(1, splits):
            @pl.when(wanted(k, h))
            def _():
                out_copy(k, h, lambda copy: copy.wait())
        return carry

    lax.fori_loop(0, stop, finish, 0)


def finish_kernel(sectors, first, width, pieces, meta, low_ref, high_ref, *refs):
    small, out_ref = refs[:pieces], refs[pieces]
    rows = out_ref.shape[1] // pieces
    for r in range(sectors):
        rank = meta[0, r]
        above = jnp.maximum(rank - first, 0)
        large = meta[1, rank] > width

        @pl.when(rank < first)
        def _():
            out_ref[r] = low_ref[jnp.minimum(rank, first - 1)].astype(jnp.float32)

        @pl.when((rank >= first) & large)
        def _():
            out_ref[r] = high_ref[above].astype(jnp.float32)

        @pl.when((rank >= first) & jnp.logical_not(large))
        def _():
            for p in range(pieces):
                out_ref[r, p * rows : (p + 1) * rows, :] = small[p][above].astype(jnp.float32)


def blank_kernel(out_ref):
    pass


ANY = pl.BlockSpec(memory_space=pl.ANY)
HBM = pl.BlockSpec(memory_space=pltpu.HBM)
SMEM = pl.BlockSpec(memory_space=pltpu.SMEM)
VMEM = pl.BlockSpec(memory_space=pltpu.VMEM)
PARAMS = pltpu.CompilerParams(vmem_limit_bytes=62 * 1024 * 1024)


def own_terms(leading, first, sectors, meta, tensor, env, other_env, splits):
    states, span, width = tensor.shape
    small = jax.ShapeDtypeStruct((sectors - first, width, width), jnp.bfloat16)
    low = jax.ShapeDtypeStruct((first, span, width), jnp.bfloat16)
    high = jax.ShapeDtypeStruct((sectors - first, span, width), jnp.bfloat16)
    products = jax.ShapeDtypeStruct((states, span, width), jnp.bfloat16)
    sems = [pltpu.SemaphoreType.DMA((splits,)), pltpu.SemaphoreType.DMA((2,))]
    if leading:
        outs = [low, high, products]
        held = (sectors, span, width)
        sems += [pltpu.SemaphoreType.DMA((sectors,)), pltpu.SemaphoreType.DMA((states + 1,))]
    else:
        outs = [small]
        held = small.shape
        sems += [pltpu.SemaphoreType.DMA((sectors - first,))]
    return pl.pallas_call(
        functools.partial(own_kernel, leading, first, sectors, states, span, width, splits),
        out_shape=outs,
        in_specs=[SMEM] + [ANY] * (2 + len(other_env)),
        out_specs=[HBM] * len(outs),
        scratch_shapes=[
            pltpu.VMEM((span, span), jnp.bfloat16),
            pltpu.VMEM((2, span, width), jnp.bfloat16),
            pltpu.VMEM((states + 1 if leading else 1, span, width), jnp.bfloat16),
            pltpu.VMEM(held, jnp.bfloat16),
        ]
        + sems,
        compiler_params=PARAMS,
        cost_estimate=pl.CostEstimate(
            flops=4 * states * span * span * width, bytes_accessed=8 * span * width, transcendentals=0
        ),
    )(meta, tensor, env, *other_env)


def other_terms(meta, low, high, products, other_tensor, states, splits):
    first, span, width = low.shape
    sectors = first + high.shape[0]
    others = max(splits - 1, 1)
    return pl.pallas_call(
        functools.partial(other_kernel, first, states, span, width, splits),
        out_shape=[jax.ShapeDtypeStruct(a.shape, jnp.bfloat16) for a in (low, high)],
        in_specs=[SMEM, HBM, HBM, ANY] + [ANY] * len(other_tensor),
        out_specs=[HBM, HBM],
        input_output_aliases={1: 0, 2: 1},
        scratch_shapes=[
            pltpu.VMEM((2, others, span, width), jnp.bfloat16),
            pltpu.VMEM((2, span, width), jnp.bfloat16),
            pltpu.VMEM((sectors, others, width, width), jnp.bfloat16),
            pltpu.SemaphoreType.DMA((2, others)),
            pltpu.SemaphoreType.DMA((2,)),
            pltpu.SemaphoreType.DMA((sectors, others)),
        ],
        compiler_params=PARAMS,
    )(meta, low, high, products, *other_tensor)


def blank(shape):
    return pl.pallas_call(
        blank_kernel, out_shape=jax.ShapeDtypeStruct(shape, jnp.bfloat16), out_specs=HBM, compiler_params=PARAMS
    )()


def line_scatter(terms, lanes):
    count, span, width = terms.shape
    chips, share = lanes // 2, span // lanes
    chip, core = lax.axis_index("charge") // 2, lax.axis_index("charge") % 2
    view = terms.reshape(count, chips, 2, share, width)
    mine = lax.dynamic_index_in_dim(view, core, 2, keepdims=False)
    theirs = lax.ppermute(
        lax.dynamic_index_in_dim(view, 1 - core, 2, keepdims=False), "charge", [(j, j ^ 1) for j in range(lanes)]
    )

    def pick(d):
        d = jnp.clip(d, 0, chips - 1)
        parts = [lax.dynamic_index_in_dim(a, d, 1, keepdims=False).astype(jnp.float32) for a in (mine, theirs)]
        return parts[0] + parts[1]

    carried = [None, None]
    for t in range(1, chips):
        values = []
        for way in range(2):
            value = pick(chips - t + chip if way == 0 else t - chips + chip)
            if carried[way] is not None:
                value = value + carried[way].astype(jnp.float32)
            values.append(value.astype(jnp.bfloat16))
        values = lax.optimization_barrier(values)
        for way in range(2):
            places = range(t) if way == 0 else range(chips - t, chips)
            hop = 1 if way == 0 else -1
            pairs = [(2 * z + c, 2 * (z + hop) + c) for z in places for c in range(2)]
            carried[way] = lax.ppermute(values[way], "charge", pairs)
    total = pick(chip)
    for part in carried:
        if part is not None:
            total = total + part.astype(jnp.float32)
    return total.astype(jnp.bfloat16)


def body(left_env, site_tensor, left_sizes, right_sizes, targets):
    splits = lax.axis_size("split")
    lanes = lax.axis_size("charge")
    tensor, env = site_tensor[0], left_env[0]
    states, span, width = tensor.shape
    sectors = right_sizes.shape[0]
    first = sectors // 2
    leads = sorted({first, max(sectors * 5 // 8, first), sectors})
    shifts = [[(y, (y + h) % splits) for y in range(splits)] for h in range(1, splits)]
    depths = max(span // TILE // (splits - 1), 1) if splits > 1 else 1
    grain = span // depths
    blocks = (left_sizes[0] + grain - 1) // grain

    groups = lax.axis_size("groups")
    other_sizes = [
        lax.ppermute(right_sizes, "groups", [(g, (g + h) % groups) for g in range(groups)]) for h in range(1, groups)
    ]

    def send_env(v):
        rows = min(v * grain, width)
        senders = -(-v * grain // width)

        def branch(block):
            piece = block[:rows, : v * grain]
            got = [lax.ppermute(piece, "split", [p for p in pairs if p[0] < senders]) for pairs in shifts]
            return tuple(jnp.pad(g, ((0, width - rows), (0, span - v * grain))) for g in got)

        return branch

    other_env = lax.switch(blocks - 1, [send_env(v) for v in range(1, depths + 1)], env)

    meta = pl.pallas_call(
        functools.partial(meta_kernel, sectors, states, width, depths, grain, leads),
        out_shape=jax.ShapeDtypeStruct((6, max(sectors, 8)), jnp.int32),
        in_specs=[SMEM] * (3 + len(other_sizes)),
        out_specs=SMEM,
    )(left_sizes, targets, right_sizes, *other_sizes)

    piece = lax.dynamic_slice(tensor, (meta[4, 0], 0, 0), (1, span, width))[0]
    slot_first = [lax.ppermute(piece, "split", pairs) for pairs in shifts]

    (small,) = own_terms(False, first, sectors, meta, tensor, env, other_env, splits)
    small, env = lax.optimization_barrier((small, env))
    small_sum = lax.psum_scatter(small, "charge", scatter_dimension=1, tiled=True)
    low, high, products = own_terms(True, first, sectors, meta, tensor, env, other_env, splits)
    low, tensor = lax.optimization_barrier((low, tensor))

    def send_tensor(used, v):
        def branch(block, meta):
            got = []
            for pairs in shifts:
                for i in range(1, states):
                    if i >= used:
                        got.append(blank((span, width)))
                        continue
                    piece = lax.dynamic_slice(block, (meta[4, i], 0, 0), (1, v * grain, width))[0]
                    got.append(jnp.pad(lax.ppermute(piece, "split", pairs), ((0, span - v * grain), (0, 0))))
            return tuple(got)

        return branch

    branches = [send_tensor(1, 1)] + [send_tensor(u, v) for u in range(2, states + 1) for v in range(1, depths + 1)]
    more = lax.switch(meta[5, 3], branches, tensor, meta)
    other_tensor = []
    for h in range(splits - 1):
        other_tensor += [slot_first[h], *more[h * (states - 1) : (h + 1) * (states - 1)]]
    low, high = other_terms(meta, low, high, products, other_tensor, states, splits)
    share = span // lanes

    def scatter(lead):
        def branch(low, high, small_sum, meta):
            low_sum = lax.psum_scatter(low, "charge", scatter_dimension=1, tiled=True)
            if lead == first:
                high_sum = blank((sectors - first, share, width))
            else:
                if lead < sectors:
                    high_sum = line_scatter(high[: lead - first], lanes)
                else:
                    high_sum = lax.psum_scatter(high, "charge", scatter_dimension=1, tiled=True)
                high_sum = jnp.pad(high_sum, ((0, sectors - lead), (0, 0), (0, 0)))
            owned = [
                lax.ppermute(small_sum, "charge", [(j, j // splits) for j in range(lanes) if j % splits == p])
                for p in range(splits)
            ]
            return pl.pallas_call(
                functools.partial(finish_kernel, sectors, first, width, splits),
                out_shape=jax.ShapeDtypeStruct((sectors, share, width), jnp.float32),
                in_specs=[SMEM] + [VMEM] * (2 + splits),
                out_specs=VMEM,
                compiler_params=PARAMS,
            )(meta, low_sum, high_sum, *owned)

        return branch

    return lax.switch(meta[5, 2], [scatter(lead) for lead in leads], low, high, small_sum, meta)


def solution(mesh):
    in_specs = (
        P(("groups", "charge"), "split", None),
        P(("groups", "charge"), None, None, "split"),
        P(("groups", "charge")),
        P("groups"),
        P(("groups", "charge"), None),
    )
    out_specs = P("groups", "charge", "split")
    return jax.shard_map(body, mesh=mesh, in_specs=in_specs, out_specs=out_specs, check_vma=False)
```

```python
import functools

import jax
import jax.numpy as jnp
from jax import lax
from jax.experimental import pallas as pl
from jax.experimental.pallas import tpu as pltpu
from jax.sharding import PartitionSpec as P

TILE = 256


def meta_kernel(sectors, states, width, depths, grain, leads, left_ref, target_ref, right_ref, *refs):
    others, out_ref = refs[:-1], refs[-1]

    def rank_sector(r, carry):
        size = right_ref[r]

        def count(other, total):
            bigger = (right_ref[other] > size) | ((right_ref[other] == size) & (other < r))
            return total + bigger.astype(jnp.int32)

        rank = lax.fori_loop(0, sectors, count, jnp.int32(0), unroll=True)
        out_ref[0, r] = rank
        out_ref[1, rank] = size
        out_ref[2, rank] = jnp.int32(-1)
        out_ref[3, rank] = jnp.int32(states)
        out_ref[4, r] = jnp.int32(0)
        out_ref[5, r] = jnp.int32(0)
        return carry

    lax.fori_loop(0, sectors, rank_sector, 0)
    for s in range(states):
        out_ref[2, out_ref[0, target_ref[0, s]]] = jnp.int32(s)

    def place(k, used):
        state = out_ref[2, k]
        wanted = (state >= 0) & (out_ref[1, k] > width)

        @pl.when(wanted)
        def _():
            out_ref[3, k] = used
            out_ref[4, used] = state

        return used + wanted.astype(jnp.int32)

    used = lax.fori_loop(0, sectors, place, jnp.int32(0))
    most = jnp.int32(0)
    for ref in (right_ref,) + others:
        def wide(r, total, ref=ref):
            return total + (ref[r] > width).astype(jnp.int32)

        most = jnp.maximum(most, lax.fori_loop(0, sectors, wide, jnp.int32(0), unroll=True))
    lead, choice = jnp.int32(leads[-1]), jnp.int32(0)
    for e in reversed(leads[:-1]):
        lead = jnp.where(most <= e, jnp.int32(e), lead)
    for e in leads[:-1]:
        choice = choice + (most > e).astype(jnp.int32)
    depth = (left_ref[0] + grain - 1) // grain
    out_ref[5, 0] = left_ref[0]
    out_ref[5, 1] = lead
    out_ref[5, 2] = choice
    out_ref[5, 3] = jnp.where(used <= 1, 0, 1 + (used - 2) * depths + depth - 1)


def own_kernel(first, sectors, states, span, width, splits, *refs):
    meta, t_hbm, own_hbm = refs[:3]
    others_e = refs[3 : 3 + splits - 1]
    small_hbm, low_hbm, high_hbm, products_hbm = refs[2 + splits : 6 + splits]
    env, mine, product, small, wide, env_sem, mine_sem, small_sem, wide_sem, product_sem = refs[6 + splits :]
    me = lax.axis_index("split")
    live_rows = meta[5, 0]
    lead = meta[5, 1]
    tiles = (live_rows + TILE - 1) // TILE

    def source_base(h):
        return pl.multiple_of(lax.rem(me - h + splits, splits) * width, width)

    env_copies = [pltpu.make_async_copy(own_hbm, env.at[pl.ds(source_base(0), width)], env_sem.at[0])] + [
        pltpu.make_async_copy(others_e[h - 1], env.at[pl.ds(source_base(h), width)], env_sem.at[h])
        for h in range(1, splits)
    ]

    def some(k):
        return (meta[2, k] >= 0) & (meta[1, k] > me * width)

    def small_wanted(k):
        return some(k) & (meta[1, k] <= width)

    def wide_wanted(k):
        return some(k) & ((k < first) | (meta[1, k] > width))

    def crossing(k):
        return some(k) & (meta[1, k] > width)

    def mine_copy(k):
        return pltpu.make_async_copy(t_hbm.at[meta[2, k]], mine.at[k % 2], mine_sem.at[k % 2])

    def begin(k, wanted):
        @pl.when(wanted(k))
        def _():
            mine_copy(k).start()

    def small_copy(k):
        return pltpu.make_async_copy(small.at[k - first], small_hbm.at[k - first], small_sem.at[k - first])

    def wide_copy(k, act):
        @pl.when(k < first)
        def _():
            act(pltpu.make_async_copy(wide.at[k], low_hbm.at[jnp.minimum(k, first - 1)], wide_sem.at[k]))

        @pl.when(k >= first)
        def _():
            act(pltpu.make_async_copy(wide.at[k], high_hbm.at[jnp.maximum(k - first, 0)], wide_sem.at[k]))

    def product_copy(k):
        return pltpu.make_async_copy(product.at[meta[3, k]], products_hbm.at[meta[3, k]], product_sem.at[meta[3, k]])

    def multiply(k, p):
        mine_copy(k).wait()
        mask(mine.at[k % 2], meta[1, k] - me * width, live_rows, width)

        def step(b, carry):
            base = pl.multiple_of(b * TILE, TILE)
            value = jnp.dot(env[pl.ds(base, TILE), :], mine[k % 2], preferred_element_type=jnp.float32)
            product[p, pl.ds(base, TILE), :] = value.astype(jnp.bfloat16)
            return carry

        def clear(b, carry):
            product[p, pl.ds(pl.multiple_of(b * TILE, TILE), TILE), :] = jnp.zeros((TILE, width), jnp.bfloat16)
            return carry

        lax.fori_loop(0, tiles, step, 0)
        lax.fori_loop(tiles, span // TILE, clear, 0)

    for copy in env_copies:
        copy.start()
    begin(first, small_wanted)
    for copy in env_copies:
        copy.wait()

    def one_small(k, carry):
        @pl.when(k + 1 < sectors)
        def _():
            begin(k + 1, small_wanted)

        @pl.when(jnp.logical_not(small_wanted(k)))
        def _():
            small[k - first] = jnp.zeros((width, width), jnp.bfloat16)

        @pl.when(small_wanted(k))
        def _():
            multiply(k, states)
            half(flat_store(small.at[k - first], 0), mine.at[k % 2], product.at[states], width)

        small_copy(k).start()
        return carry

    lax.fori_loop(first, sectors, one_small, 0)
    begin(0, wide_wanted)

    def one_wide(k, carry):
        size = meta[1, k]
        p = meta[3, k]

        @pl.when(k + 1 < lead)
        def _():
            begin(k + 1, wide_wanted)

        @pl.when(jnp.logical_not(wide_wanted(k)))
        def _():
            wide[k] = jnp.zeros(wide.shape[1:], jnp.bfloat16)

        @pl.when(wide_wanted(k))
        def _():
            multiply(k, p)
            half(flat_store(wide.at[k], me * width), mine.at[k % 2], product.at[p], width)
            for h in range(1, splits):
                @pl.when(jnp.logical_not((size > width) & (size > source_base(h))))
                def _():
                    wide[k, pl.ds(source_base(h), width), :] = jnp.zeros((width, width), jnp.bfloat16)

        wide_copy(k, lambda copy: copy.start())

        @pl.when(crossing(k))
        def _():
            product_copy(k).start()

        return carry

    lax.fori_loop(0, lead, one_wide, 0)

    def end_small(k, carry):
        small_copy(k).wait()
        return carry

    def end_wide(k, carry):
        wide_copy(k, lambda copy: copy.wait())

        @pl.when(crossing(k))
        def _():
            product_copy(k).wait()

        return carry

    lax.fori_loop(first, sectors, end_small, 0)
    lax.fori_loop(0, lead, end_wide, 0)


def mask(ref, cols, live_rows, width):
    def step(b, carry):
        base = pl.multiple_of(b * TILE, TILE)
        rows_here = lax.broadcasted_iota(jnp.int32, (TILE, width), 0) + base
        cols_here = lax.broadcasted_iota(jnp.int32, (TILE, width), 1)
        keep = (rows_here < live_rows) & (cols_here < cols)
        ref[pl.ds(base, TILE), :] = jnp.where(keep, ref[pl.ds(base, TILE), :], jnp.zeros((), jnp.bfloat16))
        return carry

    lax.fori_loop(0, ref.shape[0] // TILE, step, 0)


def flat_store(ref, row_base):
    def store(base, value):
        ref[pl.ds(pl.multiple_of(row_base + base, TILE), TILE), :] = value

    return store


def half(store, factor, product, width):
    def step(j, carry):
        base = pl.multiple_of(j * TILE, TILE)
        value = lax.dot_general(
            factor[:, pl.ds(base, TILE)], product[...], (((0,), (0,)), ((), ())), preferred_element_type=jnp.float32
        )
        store(base, value.astype(jnp.bfloat16))
        return carry

    lax.fori_loop(0, width // TILE, step, 0)


def other_kernel(first, states, span, width, splits, *refs):
    meta, products_hbm = refs[0], refs[3]
    others_t = refs[4 : 4 + (splits - 1) * states]
    low_hbm, high_hbm, theirs, product, result, theirs_sem, product_sem, out_sem = refs[4 + len(others_t) :]
    me = lax.axis_index("split")
    live_rows = meta[5, 0]
    stop = meta[5, 1]

    def source_base(h):
        return pl.multiple_of(lax.rem(me - h + splits, splits) * width, width)

    def crossing(k):
        return (meta[2, k] >= 0) & (meta[1, k] > me * width) & (meta[1, k] > width)

    def wanted(k, h):
        return crossing(k) & (meta[1, k] > source_base(h))

    def product_copy(k):
        return pltpu.make_async_copy(products_hbm.at[meta[3, k]], product.at[k % 2], product_sem.at[k % 2])

    def theirs_copy(k, h, slot):
        return pltpu.make_async_copy(others_t[(h - 1) * states + slot], theirs.at[k % 2, h - 1], theirs_sem.at[k % 2, h - 1])

    def out_copy(k, h, act):
        rows = pl.ds(source_base(h), width)

        @pl.when(k < first)
        def _():
            to = low_hbm.at[jnp.minimum(k, first - 1), rows]
            act(pltpu.make_async_copy(result.at[k, h - 1], to, out_sem.at[k, h - 1]))

        @pl.when(k >= first)
        def _():
            to = high_hbm.at[jnp.maximum(k - first, 0), rows]
            act(pltpu.make_async_copy(result.at[k, h - 1], to, out_sem.at[k, h - 1]))

    def begin(k):
        @pl.when(crossing(k))
        def _():
            product_copy(k).start()
            for slot in range(states):
                @pl.when(meta[3, k] == slot)
                def _():
                    for h in range(1, splits):
                        theirs_copy(k, h, slot).start()

    begin(0)

    def one(k, carry):
        @pl.when(k + 1 < stop)
        def _():
            begin(k + 1)

        @pl.when(crossing(k))
        def _():
            product_copy(k).wait()
            for h in range(1, splits):
                theirs_copy(k, h, 0).wait()
            for h in range(1, splits):
                @pl.when(wanted(k, h))
                def _():
                    mask(theirs.at[k % 2, h - 1], meta[1, k] - source_base(h), live_rows, width)
                    half(flat_store(result.at[k, h - 1], 0), theirs.at[k % 2, h - 1], product.at[k % 2], width)
                    out_copy(k, h, lambda copy: copy.start())

        return carry

    lax.fori_loop(0, stop, one, 0)

    def finish(k, carry):
        for h in range(1, splits):
            @pl.when(wanted(k, h))
            def _():
                out_copy(k, h, lambda copy: copy.wait())
        return carry

    lax.fori_loop(0, stop, finish, 0)


def finish_kernel(sectors, first, width, pieces, meta, low_ref, high_ref, *refs):
    small, out_ref = refs[:pieces], refs[pieces]
    rows = out_ref.shape[1] // pieces
    for r in range(sectors):
        rank = meta[0, r]
        above = jnp.maximum(rank - first, 0)
        large = meta[1, rank] > width

        @pl.when(rank < first)
        def _():
            out_ref[r] = low_ref[jnp.minimum(rank, first - 1)].astype(jnp.float32)

        @pl.when((rank >= first) & large)
        def _():
            out_ref[r] = high_ref[above].astype(jnp.float32)

        @pl.when((rank >= first) & jnp.logical_not(large))
        def _():
            for p in range(pieces):
                out_ref[r, p * rows : (p + 1) * rows, :] = small[p][above].astype(jnp.float32)


def blank_kernel(out_ref):
    pass


ANY = pl.BlockSpec(memory_space=pl.ANY)
HBM = pl.BlockSpec(memory_space=pltpu.HBM)
SMEM = pl.BlockSpec(memory_space=pltpu.SMEM)
VMEM = pl.BlockSpec(memory_space=pltpu.VMEM)
PARAMS = pltpu.CompilerParams(vmem_limit_bytes=62 * 1024 * 1024)


def own_terms(first, sectors, meta, tensor, env, other_env, splits):
    states, span, width = tensor.shape
    small = jax.ShapeDtypeStruct((sectors - first, width, width), jnp.bfloat16)
    low = jax.ShapeDtypeStruct((first, span, width), jnp.bfloat16)
    high = jax.ShapeDtypeStruct((sectors - first, span, width), jnp.bfloat16)
    products = jax.ShapeDtypeStruct((states, span, width), jnp.bfloat16)
    return pl.pallas_call(
        functools.partial(own_kernel, first, sectors, states, span, width, splits),
        out_shape=[small, low, high, products],
        in_specs=[SMEM] + [ANY] * (2 + len(other_env)),
        out_specs=[HBM] * 4,
        scratch_shapes=[
            pltpu.VMEM((span, span), jnp.bfloat16),
            pltpu.VMEM((2, span, width), jnp.bfloat16),
            pltpu.VMEM((states + 1, span, width), jnp.bfloat16),
            pltpu.VMEM(small.shape, jnp.bfloat16),
            pltpu.VMEM((sectors, span, width), jnp.bfloat16),
            pltpu.SemaphoreType.DMA((splits,)),
            pltpu.SemaphoreType.DMA((2,)),
            pltpu.SemaphoreType.DMA((sectors - first,)),
            pltpu.SemaphoreType.DMA((sectors,)),
            pltpu.SemaphoreType.DMA((states + 1,)),
        ],
        compiler_params=PARAMS,
        cost_estimate=pl.CostEstimate(
            flops=4 * states * span * span * width, bytes_accessed=8 * span * width, transcendentals=0
        ),
    )(meta, tensor, env, *other_env)


def other_terms(meta, low, high, products, other_tensor, states, splits):
    first, span, width = low.shape
    sectors = first + high.shape[0]
    others = max(splits - 1, 1)
    return pl.pallas_call(
        functools.partial(other_kernel, first, states, span, width, splits),
        out_shape=[jax.ShapeDtypeStruct(a.shape, jnp.bfloat16) for a in (low, high)],
        in_specs=[SMEM, HBM, HBM, ANY] + [ANY] * len(other_tensor),
        out_specs=[HBM, HBM],
        input_output_aliases={1: 0, 2: 1},
        scratch_shapes=[
            pltpu.VMEM((2, others, span, width), jnp.bfloat16),
            pltpu.VMEM((2, span, width), jnp.bfloat16),
            pltpu.VMEM((sectors, others, width, width), jnp.bfloat16),
            pltpu.SemaphoreType.DMA((2, others)),
            pltpu.SemaphoreType.DMA((2,)),
            pltpu.SemaphoreType.DMA((sectors, others)),
        ],
        compiler_params=PARAMS,
    )(meta, low, high, products, *other_tensor)


def blank(shape):
    return pl.pallas_call(
        blank_kernel, out_shape=jax.ShapeDtypeStruct(shape, jnp.bfloat16), out_specs=HBM, compiler_params=PARAMS
    )()


def line_scatter(terms, lanes):
    count, span, width = terms.shape
    chips, share = lanes // 2, span // lanes
    chip, core = lax.axis_index("charge") // 2, lax.axis_index("charge") % 2
    view = terms.reshape(count, chips, 2, share, width)
    mine = lax.dynamic_index_in_dim(view, core, 2, keepdims=False)
    theirs = lax.ppermute(
        lax.dynamic_index_in_dim(view, 1 - core, 2, keepdims=False), "charge", [(j, j ^ 1) for j in range(lanes)]
    )

    def pick(d):
        d = jnp.clip(d, 0, chips - 1)
        parts = [lax.dynamic_index_in_dim(a, d, 1, keepdims=False).astype(jnp.float32) for a in (mine, theirs)]
        return parts[0] + parts[1]

    carried = [None, None]
    for t in range(1, chips):
        values = []
        for way in range(2):
            value = pick(chips - t + chip if way == 0 else t - chips + chip)
            if carried[way] is not None:
                value = value + carried[way].astype(jnp.float32)
            values.append(value.astype(jnp.bfloat16))
        values = lax.optimization_barrier(values)
        for way in range(2):
            places = range(t) if way == 0 else range(chips - t, chips)
            hop = 1 if way == 0 else -1
            pairs = [(2 * z + c, 2 * (z + hop) + c) for z in places for c in range(2)]
            carried[way] = lax.ppermute(values[way], "charge", pairs)
    total = pick(chip)
    for part in carried:
        if part is not None:
            total = total + part.astype(jnp.float32)
    return total.astype(jnp.bfloat16)


def body(left_env, site_tensor, left_sizes, right_sizes, targets):
    splits = lax.axis_size("split")
    lanes = lax.axis_size("charge")
    tensor, env = site_tensor[0], left_env[0]
    states, span, width = tensor.shape
    sectors = right_sizes.shape[0]
    first = sectors // 2
    leads = sorted({first, max(sectors * 5 // 8, first), sectors})
    shifts = [[(y, (y + h) % splits) for y in range(splits)] for h in range(1, splits)]
    depths = max(span // TILE // (splits - 1), 1) if splits > 1 else 1
    grain = span // depths
    blocks = (left_sizes[0] + grain - 1) // grain

    groups = lax.axis_size("groups")
    other_sizes = [
        lax.ppermute(right_sizes, "groups", [(g, (g + h) % groups) for g in range(groups)]) for h in range(1, groups)
    ]

    def send_env(v):
        rows = min(v * grain, width)
        senders = -(-v * grain // width)

        def branch(block):
            piece = block[:rows, : v * grain]
            got = [lax.ppermute(piece, "split", [p for p in pairs if p[0] < senders]) for pairs in shifts]
            return tuple(jnp.pad(g, ((0, width - rows), (0, span - v * grain))) for g in got)

        return branch

    other_env = lax.switch(blocks - 1, [send_env(v) for v in range(1, depths + 1)], env)

    meta = pl.pallas_call(
        functools.partial(meta_kernel, sectors, states, width, depths, grain, leads),
        out_shape=jax.ShapeDtypeStruct((6, max(sectors, 8)), jnp.int32),
        in_specs=[SMEM] * (3 + len(other_sizes)),
        out_specs=SMEM,
    )(left_sizes, targets, right_sizes, *other_sizes)

    piece = lax.dynamic_slice(tensor, (meta[4, 0], 0, 0), (1, span, width))[0]
    piece, other_env = lax.optimization_barrier((piece, other_env))
    slot_first = [lax.ppermute(piece, "split", pairs) for pairs in shifts]

    small, low, high, products = own_terms(first, sectors, meta, tensor, env, other_env, splits)
    small, low, tensor, slot_first = lax.optimization_barrier((small, low, tensor, slot_first))
    small_sum = lax.psum_scatter(small, "charge", scatter_dimension=1, tiled=True)

    def send_tensor(used, v):
        def branch(block, meta):
            got = []
            for pairs in shifts:
                for i in range(1, states):
                    if i >= used:
                        got.append(blank((span, width)))
                        continue
                    piece = lax.dynamic_slice(block, (meta[4, i], 0, 0), (1, v * grain, width))[0]
                    got.append(jnp.pad(lax.ppermute(piece, "split", pairs), ((0, span - v * grain), (0, 0))))
            return tuple(got)

        return branch

    branches = [send_tensor(1, 1)] + [send_tensor(u, v) for u in range(2, states + 1) for v in range(1, depths + 1)]
    more = lax.switch(meta[5, 3], branches, tensor, meta)
    other_tensor = []
    for h in range(splits - 1):
        other_tensor += [slot_first[h], *more[h * (states - 1) : (h + 1) * (states - 1)]]
    low, high = other_terms(meta, low, high, products, other_tensor, states, splits)
    share = span // lanes

    def scatter(lead):
        def branch(low, high, small_sum, meta):
            low_sum = lax.psum_scatter(low, "charge", scatter_dimension=1, tiled=True)
            if lead == first:
                high_sum = blank((sectors - first, share, width))
            else:
                if lead < sectors:
                    high_sum = line_scatter(high[: lead - first], lanes)
                else:
                    high_sum = lax.psum_scatter(high, "charge", scatter_dimension=1, tiled=True)
                high_sum = jnp.pad(high_sum, ((0, sectors - lead), (0, 0), (0, 0)))
            owned = [
                lax.ppermute(small_sum, "charge", [(j, j // splits) for j in range(lanes) if j % splits == p])
                for p in range(splits)
            ]
            return pl.pallas_call(
                functools.partial(finish_kernel, sectors, first, width, splits),
                out_shape=jax.ShapeDtypeStruct((sectors, share, width), jnp.float32),
                in_specs=[SMEM] + [VMEM] * (2 + splits),
                out_specs=VMEM,
                compiler_params=PARAMS,
            )(meta, low_sum, high_sum, *owned)

        return branch

    return lax.switch(meta[5, 2], [scatter(lead) for lead in leads], low, high, small_sum, meta)


def solution(mesh):
    in_specs = (
        P(("groups", "charge"), "split", None),
        P(("groups", "charge"), None, None, "split"),
        P(("groups", "charge")),
        P("groups"),
        P(("groups", "charge"), None),
    )
    out_specs = P("groups", "charge", "split")
    return jax.shard_map(body, mesh=mesh, in_specs=in_specs, out_specs=out_specs, check_vma=False)
```
